32 devices in a mesh: groups: 2 (over y), clus: 4 (over z), sub: 2 (over x), rep: 2 (over core).
Axes of the slice: x: 2, y: 2, z: 4, core: 2. Of those that a mesh axis runs over, the one named last changes fastest.
Arguments:
- embeds: bfloat16 [16384, 768], P(('groups', 'clus', 'sub', 'rep')), parts along dimension 0
- cluster_of: int32 [16384], P(('groups', 'clus', 'sub', 'rep')), parts along dimension 0, may hold values from 0 to 7, as said below
- order_in: int32 [16384], P(('groups', 'clus', 'sub', 'rep')), parts along dimension 0, may hold values from 0 to 1023, as said below
- partner: int32 [16], P(('groups', 'clus', 'sub')), parts along dimension 0, may hold values from 0 to 7, as said below
- border_idx: int32 [16, 256], P(('groups', 'clus', 'sub')), parts along dimension 0, may hold values from 0 to 1023, as said below
Outputs:
- log_weight: float32 [16384], P(('groups', 'clus', 'sub', 'rep')), parts along dimension 0
The draws below stay inside these ranges and needn't reach their ends.
There are 2 independent parts, one for each index of `groups`. The reference program is written for one: setup_inputs(seed, part) draws one part's arguments, and reference() takes and returns one part's arrays. A program takes and returns all parts, laid end to end along the dimension named above; each array names one. Nothing has to cross between parts.
Inputs may be any that keep to these rules, and one draw needn't show every extreme that they name: `cluster_of`: row blocks of 512 rows, in order, belong to the devices in the order of clus, sub, rep (rep fastest). Every cluster number is named by exactly 1024 rows. The owner of cluster c is c. Of the rows of one block, at most 128 name clusters of one owner, and in every draw some block has exactly 128 rows for some owner. `order_in`: the 1024 rows of one cluster have distinct positions; rows with a position below 512 lie in blocks of rep index 0, the others in blocks of rep index 1. partner[c] // 1 equals (c + 4) modulo 4 * 2. `border_idx`: the 256 positions of one cluster are distinct.
All inputs are finite; a program needn't handle non-finite values.
Results may differ from the reference program's by a relative error of at most 0.0003.
Values may be sent and summed in bfloat16 or wider, within the bound.
No kernel may reach another device: no remote copies, remote signals or barrier semaphores. Data moves between devices by JAX's collectives and lax.ppermute only.
A program may use at most 64 MiB of HBM per device.

```python
import math
import jax
import jax.numpy as jnp
from jax import lax

D = 768
CL_DEV = 1
CAP = 1024
BORDER = 256
ROW_DEV = 512
NCL = 8
ROWS = 8192
N_CLUS = 4
N_SUB = 2
N_REP = 2


def routed_row_set(key):
    owners = N_CLUS * N_SUB
    mean_rows = ROW_DEV // owners
    half = CAP // 2
    cluster_parts = []
    order_parts = []
    for side in range(N_REP):
        keys = jax.random.split(jax.random.fold_in(key, 101 + side), 6)
        shuffle = jax.random.permutation(keys[0], owners).astype(jnp.int32)
        amounts = jax.random.randint(keys[1], (owners // 2,), 0, mean_rows + 1).astype(jnp.int32)
        amounts = amounts.at[0].set(mean_rows)
        counts = jnp.full((owners,), mean_rows, jnp.int32)
        counts = counts.at[shuffle[:owners // 2]].add(amounts).at[shuffle[owners // 2:]].add(-amounts)
        sigma = jax.random.permutation(keys[2], owners).astype(jnp.int32)
        pi_perm = jax.random.permutation(keys[3], owners).astype(jnp.int32)
        inverse = jnp.zeros((owners,), jnp.int32).at[pi_perm].set(jnp.arange(owners, dtype=jnp.int32))
        shifts = jnp.repeat(jnp.arange(owners, dtype=jnp.int32), counts, total_repeat_length=ROW_DEV)
        starts = jnp.cumsum(counts) - counts
        rank = jnp.arange(ROW_DEV, dtype=jnp.int32) - starts[shifts]
        target_rows = inverse[(sigma[:, None] + shifts[None, :]) % owners]
        matrix = counts[(pi_perm[None, :] - sigma[:, None]) % owners]
        offset = jnp.cumsum(matrix, axis=0) - matrix
        arrival = offset[jnp.arange(owners, dtype=jnp.int32)[:, None], target_rows] + rank[None, :]
        layout = jax.vmap(lambda sub_key: jax.random.permutation(sub_key, ROW_DEV))(jax.random.split(keys[4], owners)).astype(jnp.int32)
        local = layout[target_rows, arrival]
        cluster = target_rows * CL_DEV + local // half
        order = side * half + local % half
        mixing = jax.vmap(lambda sub_key: jax.random.permutation(sub_key, ROW_DEV))(jax.random.split(keys[5], owners)).astype(jnp.int32)
        cluster_parts.append(jnp.take_along_axis(cluster, mixing, axis=1))
        order_parts.append(jnp.take_along_axis(order, mixing, axis=1))
    cluster_all = jnp.stack(cluster_parts, axis=1).reshape(-1).astype(jnp.int32)
    order_all = jnp.stack(order_parts, axis=1).reshape(-1).astype(jnp.int32)
    return (cluster_all, order_all)


def log_uniform(key, shape, low, high):
    return jnp.exp(jax.random.uniform(key, shape, jnp.float32, math.log(low), math.log(high)))


def make_image_codes(key, cluster, noise, along, scales):
    keys = jax.random.split(key, 4)
    common = jax.random.normal(keys[0], (D,), jnp.float32)
    centers = jax.random.normal(keys[1], (NCL, D), jnp.float32)
    strength = log_uniform(keys[2], (NCL,), 0.3, 1.5)
    feature_vectors = log_uniform(keys[3], (D,), 0.4, 2.5)
    mixed = strength[cluster][:, None] * common[None, :] + 0.4 * centers[cluster]
    values = scales[:, None] * feature_vectors[None, :] * (along[:, None] * mixed + noise)
    return values.astype(jnp.bfloat16)


def draw_embeds(key, part):
    cluster, order = routed_row_set(key)
    key = jax.random.fold_in(key, 7)
    keys = jax.random.split(key, 4)
    noise = jax.random.normal(keys[0], (ROWS, D), jnp.float32)
    along = log_uniform(keys[1], (ROWS,), 0.3, 1.5)
    scales = log_uniform(keys[2], (ROWS,), 0.5, 5.0)
    return make_image_codes(keys[3], cluster, noise, along, scales)


def draw_cluster_of(key, part):
    cluster, order = routed_row_set(key)
    return cluster


def draw_order_in(key, part):
    cluster, order = routed_row_set(key)
    return order


def draw_partner(key, part):
    key = jax.random.fold_in(key, 3)
    owners = N_CLUS * N_SUB
    index = jnp.arange(NCL, dtype=jnp.int32)
    facing = (index // CL_DEV + N_SUB * (N_CLUS // 2)) % owners
    local = jax.random.randint(key, (NCL,), 0, CL_DEV).astype(jnp.int32)
    return (facing * CL_DEV + local).astype(jnp.int32)


def draw_border_idx(key, part):
    key = jax.random.fold_in(key, 5)
    picks = jax.vmap(lambda sub_key: jax.random.permutation(sub_key, CAP)[:BORDER])(jax.random.split(key, NCL))
    return picks.astype(jnp.int32)


def setup_inputs(seed: int = 0, part: int = 0) -> dict:
    seeds = jax.random.split(jax.random.key(seed), 6)
    part_keys = jax.random.split(jax.random.fold_in(seeds[5], part), 6)
    return {
        "embeds": draw_embeds(jax.random.fold_in(jax.random.fold_in(seeds[5], part), 71), part),
        "cluster_of": draw_cluster_of(jax.random.fold_in(jax.random.fold_in(seeds[5], part), 71), part),
        "order_in": draw_order_in(jax.random.fold_in(jax.random.fold_in(seeds[5], part), 71), part),
        "partner": draw_partner(jax.random.fold_in(jax.random.fold_in(seeds[5], part), 71), part),
        "border_idx": draw_border_idx(jax.random.fold_in(jax.random.fold_in(seeds[5], part), 71), part),
    }


smoothing_scale = 0.1

def reference(embeds, cluster_of, order_in, partner, border_idx):
    values = embeds.astype(jnp.float32)
    unit = (values * lax.rsqrt(lax.optimization_barrier(jnp.mean(values * values, axis=1, keepdims=True)) + 1e-06)).astype(jnp.bfloat16)
    flat = (cluster_of * CAP + order_in).astype(jnp.int32)
    members = jnp.zeros((NCL * CAP, D), jnp.bfloat16).at[flat].set(unit).reshape(NCL, CAP, D)
    slots = jnp.arange(CAP, dtype=jnp.int32)

    def one_cluster(index):
        rows = members[index]
        other = partner[index]
        tile = jnp.take(members[other], border_idx[other], axis=0)
        adjacent_partition = jnp.dot(rows, rows.T, preferred_element_type=jnp.float32) / D
        importance_function = jnp.exp((adjacent_partition - 1.0) / smoothing_scale)
        importance_function = jnp.where(slots[:, None] == slots[None, :], jnp.float32(0.0), importance_function)
        remote_partition = jnp.dot(rows, tile.T, preferred_element_type=jnp.float32) / D
        summed_importance = lax.optimization_barrier(jnp.sum(importance_function, axis=1)) + lax.optimization_barrier(jnp.sum(jnp.exp((remote_partition - 1.0) / smoothing_scale), axis=1))
        return -jnp.log(summed_importance / (CAP - 1 + BORDER))
    result = lax.map(one_cluster, jnp.arange(NCL, dtype=jnp.int32))
    return result.reshape(-1)[flat]
```

```python
import functools

import jax
import jax.numpy as jnp
from jax import lax
from jax.experimental import pallas as pl
from jax.experimental.pallas import tpu as pltpu
from jax.sharding import PartitionSpec as P

CAP = 1024
HALF = CAP // 2
BORDER = 256
EPS = 1e-06
SCALE = 0.1
LANES = 128
EMPTY = 4096
OWNERS = ("clus", "sub")

ROWS_BY_ROWS = (((1,), (1,)), ((), ()))
COLS_BY_COLS = (((0,), (0,)), ((), ()))


def dot(a, b, dims=(((1,), (0,)), ((), ())), precision=None):
    return lax.dot_general(
        a, b, dims, precision=precision, preferred_element_type=jnp.float32
    )


def call(body, out_shape, flops, *args):
    moved = sum(a.size * a.dtype.itemsize for a in args)
    moved += sum(o.size * o.dtype.itemsize for o in jax.tree.leaves(out_shape))
    spec = pl.BlockSpec(memory_space=pltpu.VMEM)
    many = isinstance(out_shape, (list, tuple))
    return pl.pallas_call(
        body,
        out_shape=out_shape,
        in_specs=[spec] * len(args),
        out_specs=[spec] * len(out_shape) if many else spec,
        compiler_params=pltpu.CompilerParams(vmem_limit_bytes=40 * 2**20),
        cost_estimate=pl.CostEstimate(flops=flops, bytes_accessed=moved, transcendentals=0),
    )(*args)


def iota(shape, axis):
    return lax.broadcasted_iota(jnp.int32, shape, axis)


def one_hot(condition):
    return jnp.where(condition, 1.0, 0.0).astype(jnp.bfloat16)


def pack_body(owners, send, embeds_ref, owner_ref, *outs):
    rows, width = embeds_ref.shape
    values = embeds_ref[...].astype(jnp.float32)
    mean = jnp.sum(values * values, axis=1, keepdims=True) / width
    unit = (values * lax.rsqrt(mean + EPS)).astype(jnp.bfloat16)
    owner = owner_ref[...]
    which = iota((max(owners, 16), rows), 0) == owner
    before = one_hot(iota((rows, rows), 0) < iota((rows, rows), 1))
    counts = dot(one_hot(which), before)
    rank = jnp.sum(jnp.where(which, counts, 0.0), axis=0, keepdims=True)
    place = owner * send + rank.astype(jnp.int32)
    per = owners * send // len(outs)
    for n, out in enumerate(outs):
        chosen = one_hot(iota((per, rows), 0) + n * per == place)
        out[...] = dot(chosen, unit).astype(jnp.bfloat16)


def border_body(count, *refs):
    chunks, (tags_ref, want_ref, keep_ref, give_ref) = refs[:count], refs[count:]
    incoming = jnp.concatenate([c[...] for c in chunks], axis=0)
    chosen = one_hot(want_ref[...] == tags_ref[...])
    picked = dot(chosen, incoming).astype(jnp.bfloat16)
    keep_ref[...] = picked[: BORDER // 2]
    give_ref[...] = picked[BORDER // 2 :]


def place_body(count, *refs):
    chunks, (tags_ref, mine_ref) = refs[:count], refs[count:]
    incoming = jnp.concatenate([c[...] for c in chunks], axis=0)
    chosen = one_hot(iota((HALF, incoming.shape[0]), 0) == tags_ref[...])
    mine_ref[...] = dot(chosen, incoming).astype(jnp.bfloat16)


def weigh(products, width):
    return jnp.exp((products / width - 1.0) / SCALE)


def near_body(mine_ref, other_ref, near_ref):
    mine, other = mine_ref[...], other_ref[...]
    width = mine.shape[1]
    own = weigh(dot(mine, mine, ROWS_BY_ROWS), width)
    own = jnp.where(iota(own.shape, 0) == iota(own.shape, 1), 0.0, own)
    across = weigh(dot(other, mine, ROWS_BY_ROWS), width)
    near_ref[...] = jnp.sum(own, axis=0, keepdims=True) + jnp.sum(across, axis=0, keepdims=True)


def far_body(mine_ref, first_ref, second_ref, near_ref, scores_ref):
    mine = mine_ref[...]
    width = mine.shape[1]
    total = near_ref[...]
    for tile in (first_ref, second_ref):
        far = weigh(dot(tile[...], mine, ROWS_BY_ROWS), width)
        total = total + jnp.sum(far, axis=0, keepdims=True)
    scores = -jnp.log(total / (CAP - 1 + BORDER))
    for r in range(HALF // LANES):
        scores_ref[r : r + 1, :] = scores[:, r * LANES : (r + 1) * LANES]


def answer_body(scores_ref, where_ref, out_ref):
    scores, where = scores_ref[...], where_ref[...]
    lines, rows = scores.shape[0], where.shape[1]
    line = jnp.where(iota((lines, rows), 0) == where // LANES, 1.0, 0.0)
    found = dot(scores, line, COLS_BY_COLS, precision=lax.Precision.HIGHEST)
    lane = iota((LANES, rows), 0) == where % LANES
    out_ref[...] = jnp.sum(jnp.where(lane, found, 0.0), axis=0, keepdims=True)


def per_device(embeds, cluster_of, order_in, partner, border_idx):
    rows, width = embeds.shape
    clus_count = lax.axis_size("clus")
    owners = clus_count * lax.axis_size("sub")
    send = 2 * rows // owners
    me = lax.axis_index(OWNERS)
    side = lax.axis_index("rep")
    swap = [(0, 1), (1, 0)]
    paired = owners <= 8

    def toward(x, flip):
        return lax.ppermute(x, OWNERS, [(i, i ^ flip) for i in range(owners)])

    def gather(x):
        if not paired:
            return lax.all_gather(x, OWNERS, axis=0, tiled=True)
        flip = 1
        while flip < owners:
            x = jnp.concatenate([x, toward(x, flip)], axis=0)
            flip *= 2
        return x

    base = me if paired else jnp.zeros_like(me)
    owner = cluster_of ^ base
    chunk_count = owners if paired else 1
    chunk = jax.ShapeDtypeStruct((owners * send // chunk_count, width), jnp.bfloat16)
    chunks = call(
        functools.partial(pack_body, owners, send),
        [chunk] * chunk_count,
        2 * owners * send * rows * width,
        embeds,
        owner.reshape(1, rows),
    )
    if paired:
        order = [4, 6, 1, 2, 3, 5, 7] if owners == 8 else range(1, owners)
        got = {k: toward(chunks[k], k) for k in order}
        got[0] = chunks[0]
        chunks = [got[k] for k in range(owners)]
    else:
        blocks = chunks[0].reshape(owners, send, width)
        blocks = lax.all_to_all(blocks, OWNERS, split_axis=0, concat_axis=0, tiled=True)
        chunks = [blocks.reshape(owners * send, width)]

    every = gather((cluster_of * CAP + order_in).reshape(rows // LANES, LANES))
    every = every.reshape(owners, rows)
    mask = (every // CAP) == me
    upto = (
        jnp.arange(rows, dtype=jnp.int32)[:, None] < jnp.arange(rows, dtype=jnp.int32)[None, :]
    ).astype(jnp.bfloat16)
    rank = dot(mask.astype(jnp.bfloat16), upto).astype(jnp.int32)
    rank = jnp.where(mask, rank, -1)
    hit = rank[:, None, :] == jnp.arange(send, dtype=jnp.int32)[None, :, None]
    tags = jnp.sum(jnp.where(hit, (every % HALF - EMPTY)[:, None, :], 0), axis=2) + EMPTY
    tags = tags.reshape(1, owners * send)

    want = border_idx.reshape(BORDER, 1) - side * HALF
    want = jnp.where(side == 0, want, jnp.roll(want, BORDER // 2, axis=0))
    part = jax.ShapeDtypeStruct((BORDER // 2, width), jnp.bfloat16)
    keep, give = call(
        functools.partial(border_body, len(chunks)),
        [part, part],
        2 * BORDER * owners * send * width,
        *chunks,
        tags,
        want,
    )
    chosen = keep + lax.ppermute(give, "rep", swap)
    by = clus_count // 2
    first = lax.ppermute(chosen, "clus", [(i, (i + by) % clus_count) for i in range(clus_count)])
    mine = call(
        functools.partial(place_body, len(chunks)),
        jax.ShapeDtypeStruct((HALF, width), jnp.bfloat16),
        2 * HALF * owners * send * width,
        *chunks,
        tags,
    )
    other = lax.ppermute(mine, "rep", swap)
    near = call(
        near_body,
        jax.ShapeDtypeStruct((1, HALF), jnp.float32),
        2 * HALF * CAP * width,
        mine,
        other,
    )
    second = lax.ppermute(first, "rep", swap)
    scores = call(
        far_body,
        jax.ShapeDtypeStruct((HALF // LANES, LANES), jnp.float32),
        2 * HALF * BORDER * width,
        mine,
        first,
        second,
        near,
    )
    where = owner * HALF + order_in % HALF
    answers = call(
        answer_body,
        jax.ShapeDtypeStruct((1, rows), jnp.float32),
        2 * owners * HALF * rows,
        gather(scores),
        where.reshape(1, rows),
    )
    return answers.reshape(rows)


def solution(mesh):
    return jax.shard_map(
        per_device,
        mesh=mesh,
        in_specs=(
            P(("groups", "clus", "sub", "rep"), None),
            P(("groups", "clus", "sub", "rep")),
            P(("groups", "clus", "sub", "rep")),
            P(("groups", "clus", "sub")),
            P(("groups", "clus", "sub"), None),
        ),
        out_specs=P(("groups", "clus", "sub", "rep")),
        check_vma=False,
    )
```

```python
import functools

import jax
import jax.numpy as jnp
from jax import lax
from jax.experimental import pallas as pl
from jax.experimental.pallas import tpu as pltpu
from jax.sharding import PartitionSpec as P

CAP = 1024
HALF = CAP // 2
BORDER = 256
EPS = 1e-06
SCALE = 0.1
LANES = 128
TAG_ROWS = 8
TAG_BASE = 32
EMPTY = 4096
PIECES = 4
OWNERS = ("clus", "sub")

ROWS_BY_ROWS = (((1,), (1,)), ((), ()))


def dot(a, b, dims=(((1,), (0,)), ((), ()))):
    return lax.dot_general(a, b, dims, preferred_element_type=jnp.float32)


def call(body, out_shape, flops, *args, after=()):
    leaves, tree = jax.tree.flatten(args)
    moved = sum(a.size * a.dtype.itemsize for a in leaves)
    moved += sum(o.size * o.dtype.itemsize for o in jax.tree.leaves(out_shape))
    spec = pl.BlockSpec(memory_space=pltpu.VMEM)
    many = isinstance(out_shape, (list, tuple))
    count = len(leaves)

    def kernel(*refs):
        body(*jax.tree.unflatten(tree, refs[:count]), *refs[count + len(after) :])

    return pl.pallas_call(
        kernel,
        out_shape=out_shape,
        in_specs=[spec] * count + [pl.BlockSpec(memory_space=pl.ANY)] * len(after),
        out_specs=[spec] * len(out_shape) if many else spec,
        compiler_params=pltpu.CompilerParams(vmem_limit_bytes=40 * 2**20),
        cost_estimate=pl.CostEstimate(flops=flops, bytes_accessed=moved, transcendentals=0),
    )(*leaves, *after)


def iota(shape, axis):
    return lax.broadcasted_iota(jnp.int32, shape, axis)


def one_hot(condition):
    return jnp.where(condition, 1.0, 0.0).astype(jnp.bfloat16)


TAGS = {
    0: ((0,), ()),
    1: ((1, 3, 5, 7), ()),
    2: ((2, 6), ((1, 1), (1, 3))),
    4: ((4,), ((1, 2), (2, 1), (2, 3))),
}
TAG_LINE = ((0, 0), (1, 0), (2, 0), (2, 2), (4, 0), (4, 1), (4, 2), (4, 3))
STEPS = (((7, 6, 1, 3, 0), ()), ((2, 5), (1,)), ((4,), (1, 2)))


def pack(send, blocks, unit, place, position, arrived, outs):
    rows, width = unit.shape
    parts = jnp.where(iota((16, rows), 0) == 0, position // TAG_BASE, position % TAG_BASE)
    parts = parts.astype(jnp.float32).astype(jnp.bfloat16)

    def chosen(block):
        return one_hot(iota((send, rows), 0) + block * send == place)

    def tag_line(block):
        found = dot(parts, chosen(block), ROWS_BY_ROWS)
        return jnp.concatenate([found[0:1], found[1:2]], axis=1)

    for block, out in zip(blocks, outs):
        out[:send, :] = dot(chosen(block), unit).astype(jnp.bfloat16)
        if block in TAGS:
            own, handed = TAGS[block]
            lines = [tag_line(b) for b in own]
            lines += [arrived[c][send:, : 2 * send][n : n + 1] for c, n in handed]
            lines = [line.astype(jnp.float32) for line in lines]
            lines.append(jnp.zeros((TAG_ROWS - len(lines), 2 * send), jnp.float32))
            lines = jnp.concatenate(lines, axis=0)
            rest = jnp.zeros((TAG_ROWS, width - 2 * send), jnp.float32)
            out[send:, :] = jnp.concatenate([lines, rest], axis=1).astype(jnp.bfloat16)


def rank_body(owners, send, cluster_ref, base_ref, place_ref):
    rows = cluster_ref.shape[1]
    owner = cluster_ref[...] ^ base_ref[...]
    which = iota((max(owners, 16), rows), 0) == owner
    before = one_hot(iota((rows, rows), 0) < iota((rows, rows), 1))
    counts = dot(one_hot(which), before)
    rank = jnp.sum(jnp.where(which, counts, 0.0), axis=0, keepdims=True)
    place_ref[...] = owner * send + rank.astype(jnp.int32)


def first_body(send, blocks, embeds_ref, place_ref, order_ref, unit_ref, *outs):
    values = embeds_ref[...].astype(jnp.float32)
    mean = jnp.sum(values * values, axis=1, keepdims=True) / values.shape[1]
    unit = (values * lax.rsqrt(mean + EPS)).astype(jnp.bfloat16)
    unit_ref[...] = unit
    place = place_ref[...]
    if blocks:
        pack(send, blocks, unit, place, order_ref[...] % HALF + 1, {}, outs)
    else:
        (out,) = outs
        chosen = one_hot(iota((out.shape[0], place.shape[1]), 0) == place)
        out[...] = dot(chosen, unit).astype(jnp.bfloat16)


def pack_body(send, blocks, unit_ref, place_ref, order_ref, arrived, *outs):
    position = order_ref[...] % HALF + 1
    pack(send, blocks, unit_ref[...], place_ref[...], position, arrived, outs)


def tags_of(chunks, tags, send):
    if tags:
        return tags[0][...]
    found = []
    for chunk, line in TAG_LINE:
        lines = chunks[chunk][send:, : 2 * send].astype(jnp.float32)[line : line + 1]
        found.append(lines[:, :send] * TAG_BASE + lines[:, send:])
    found = jnp.concatenate(found, axis=1).astype(jnp.int32)
    return jnp.where(found == 0, EMPTY, found - 1)


def rows_of(chunks, send):
    if 1 not in chunks:
        return chunks[0][...]
    return jnp.concatenate([chunks[k][:send, :] for k in range(8)], axis=0)


def border_body(send, chunks, want_ref, tags, keep_ref, give_ref):
    chosen = one_hot(want_ref[...] == tags_of(chunks, tags, send))
    picked = dot(chosen, rows_of(chunks, send)).astype(jnp.bfloat16)
    keep_ref[...] = picked[: BORDER // 2]
    give_ref[...] = picked[BORDER // 2 :]


def place_body(send, chunks, tags, *mine_refs):
    tags = tags_of(chunks, tags, send)
    rows = rows_of(chunks, send)
    first = 0
    for mine_ref in mine_refs:
        count = mine_ref.shape[0]
        chosen = one_hot(iota((count, tags.shape[1]), 0) + first == tags)
        mine_ref[...] = dot(chosen, rows).astype(jnp.bfloat16)
        first += count


def weigh(products, width):
    return jnp.exp((products / width - 1.0) / SCALE)


def near_body(mine_refs, other_refs, near_ref):
    mine = jnp.concatenate([ref[...] for ref in mine_refs], axis=0)
    other = jnp.concatenate([ref[...] for ref in other_refs], axis=0)
    width = mine.shape[1]
    own = weigh(dot(mine, mine, ROWS_BY_ROWS), width)
    own = jnp.where(iota(own.shape, 0) == iota(own.shape, 1), 0.0, own)
    across = weigh(dot(other, mine, ROWS_BY_ROWS), width)
    near_ref[...] = jnp.sum(own, axis=0, keepdims=True) + jnp.sum(across, axis=0, keepdims=True)


def far_body(mine_refs, other_refs, tile_ref, near_ref, here_ref, there_ref):
    tile = tile_ref[...]
    for rows_refs, out_ref in ((mine_refs, here_ref), (other_refs, there_ref)):
        rows = jnp.concatenate([ref[...] for ref in rows_refs], axis=0)
        far = weigh(dot(tile, rows, ROWS_BY_ROWS), tile.shape[1])
        total = jnp.sum(far, axis=0, keepdims=True)
        if out_ref is here_ref:
            total = total + near_ref[...]
        for r in range(HALF // LANES):
            out_ref[r : r + 1, :] = total[:, r * LANES : (r + 1) * LANES]


def answer_body(scores_ref, cluster_ref, order_ref, base_ref, out_ref):
    lines_each = HALF // LANES
    place = order_ref[...] % HALF
    line = (cluster_ref[...] ^ base_ref[...]) * lines_each + place // LANES
    lane = place % LANES

    def add(n, found):
        scores = jnp.broadcast_to(scores_ref[pl.ds(n, 1), :], lane.shape)
        there = jnp.take_along_axis(scores, lane, axis=1)
        return jnp.where(line == n, there, found)

    lines = scores_ref.shape[0]
    found = jnp.zeros(lane.shape, jnp.float32)
    out_ref[...] = lax.fori_loop(0, lines, add, found, unroll=lines <= 64)


def per_device(embeds, cluster_of, order_in, partner, border_idx):
    rows, width = embeds.shape
    clus_count = lax.axis_size("clus")
    owners = clus_count * lax.axis_size("sub")
    send = 2 * rows // owners
    me = lax.axis_index(OWNERS)
    side = lax.axis_index("rep")
    swap = [(0, 1), (1, 0)]
    paired = owners == 8

    def toward(x, flip):
        return lax.ppermute(x, OWNERS, [(i, i ^ flip) for i in range(owners)])

    def gather(x):
        if not paired:
            return lax.all_gather(x, OWNERS, axis=0, tiled=True)
        for flip in (1, 2, 4):
            x = jnp.concatenate([x, toward(x, flip)], axis=0)
        return x

    base = me if paired else jnp.zeros_like(me)
    base = base.reshape(1, 1)
    cluster_row = cluster_of.reshape(1, rows)
    order_row = order_in.reshape(1, rows)

    def shapes(blocks):
        sizes = [(send + TAG_ROWS * (b in TAGS), width) for b in blocks] or [(owners * send, width)]
        return [jax.ShapeDtypeStruct(size, jnp.bfloat16) for size in sizes]

    place = call(
        functools.partial(rank_body, owners, send),
        jax.ShapeDtypeStruct((1, rows), jnp.int32),
        2 * owners * rows * rows,
        cluster_row,
        base,
    )

    def first(blocks):
        return call(
            functools.partial(first_body, send, blocks),
            [jax.ShapeDtypeStruct((rows, width), jnp.bfloat16), *shapes(blocks)],
            2 * rows * rows * width,
            embeds,
            place,
            order_row,
        )

    if paired:
        chunks = {}
        for blocks, needed in STEPS:
            if not chunks:
                unit, *packed = first(blocks)
            else:
                handed = {k: chunks[k] for k in needed}
                packed = call(
                    functools.partial(pack_body, send, blocks),
                    shapes(blocks),
                    2 * len(blocks) * send * rows * width,
                    unit,
                    place,
                    order_row,
                    handed,
                )
            for block, chunk in zip(blocks, packed):
                chunks[block] = toward(chunk, block) if block else chunk
        tags = []
    else:
        _, blocks = first(())
        blocks = blocks.reshape(owners, send, width)
        blocks = lax.all_to_all(blocks, OWNERS, split_axis=0, concat_axis=0, tiled=True)
        chunks = {0: blocks.reshape(owners * send, width)}
        every = gather(cluster_of * CAP + order_in).reshape(owners, rows)
        mask = (every // CAP) == me
        index = jnp.arange(rows, dtype=jnp.int32)
        before = (index[:, None] < index[None, :]).astype(jnp.bfloat16)
        rank = dot(mask.astype(jnp.bfloat16), before).astype(jnp.int32)
        rank = jnp.where(mask, rank, -1)
        hit = rank[:, None, :] == index[None, :send, None]
        found = jnp.sum(jnp.where(hit, (every % HALF - EMPTY)[:, None, :], 0), axis=2) + EMPTY
        tags = [found.reshape(1, owners * send)]

    want = border_idx.reshape(BORDER, 1) - side * HALF
    want = jnp.where(side == 0, want, jnp.roll(want, BORDER // 2, axis=0))
    by = clus_count // 2
    across = [(i, (i + by) % clus_count) for i in range(clus_count)]
    part = jax.ShapeDtypeStruct((BORDER // 2, width), jnp.bfloat16)
    keep, give = call(
        functools.partial(border_body, send),
        [part, part],
        2 * BORDER * owners * send * width,
        chunks,
        want,
        tags,
    )
    tile = lax.ppermute(keep + lax.ppermute(give, "rep", swap), "clus", across)
    part = jax.ShapeDtypeStruct((HALF // PIECES, width), jnp.bfloat16)
    mine = call(
        functools.partial(place_body, send),
        [part] * PIECES,
        2 * HALF * owners * send * width,
        chunks,
        tags,
        after=[give],
    )
    other = [lax.ppermute(part, "rep", swap) for part in mine]
    near = call(
        near_body,
        jax.ShapeDtypeStruct((1, HALF), jnp.float32),
        2 * HALF * CAP * width,
        mine,
        other,
    )
    lines = jax.ShapeDtypeStruct((HALF // LANES, LANES), jnp.float32)
    here, there = call(
        far_body,
        [lines, lines],
        2 * HALF * BORDER * width,
        mine,
        other,
        tile,
        near,
    )
    total = here + lax.ppermute(there, "rep", swap)
    scores = -jnp.log(total / (CAP - 1 + BORDER))
    answers = call(
        answer_body,
        jax.ShapeDtypeStruct((rows // LANES, LANES), jnp.float32),
        owners * HALF,
        gather(scores),
        cluster_of.reshape(rows // LANES, LANES),
        order_in.reshape(rows // LANES, LANES),
        base,
    )
    return answers.reshape(rows)


def solution(mesh):
    return jax.shard_map(
        per_device,
        mesh=mesh,
        in_specs=(
            P(("groups", "clus", "sub", "rep"), None),
            P(("groups", "clus", "sub", "rep")),
            P(("groups", "clus", "sub", "rep")),
            P(("groups", "clus", "sub")),
            P(("groups", "clus", "sub"), None),
        ),
        out_specs=P(("groups", "clus", "sub", "rep")),
        check_vma=False,
    )
```

```python
import functools

import jax
import jax.numpy as jnp
from jax import lax
from jax.experimental import pallas as pl
from jax.experimental.pallas import tpu as pltpu
from jax.sharding import PartitionSpec as P

CAP = 1024
HALF = CAP // 2
BORDER = 256
EPS = 1e-06
SCALE = 0.1
LANES = 128
TAG_ROWS = 8
TAG_BASE = 32
EMPTY = 4096
PIECES = 4
OWNERS = ("clus", "sub")

ROWS_BY_ROWS = (((1,), (1,)), ((), ()))


def dot(a, b, dims=(((1,), (0,)), ((), ()))):
    return lax.dot_general(a, b, dims, preferred_element_type=jnp.float32)


def call(body, out_shape, flops, *args, after=()):
    leaves, tree = jax.tree.flatten(args)
    moved = sum(a.size * a.dtype.itemsize for a in leaves)
    moved += sum(o.size * o.dtype.itemsize for o in jax.tree.leaves(out_shape))
    spec = pl.BlockSpec(memory_space=pltpu.VMEM)
    many = isinstance(out_shape, (list, tuple))
    count = len(leaves)

    def kernel(*refs):
        body(*jax.tree.unflatten(tree, refs[:count]), *refs[count + len(after) :])

    return pl.pallas_call(
        kernel,
        out_shape=out_shape,
        in_specs=[spec] * count + [pl.BlockSpec(memory_space=pl.ANY)] * len(after),
        out_specs=[spec] * len(out_shape) if many else spec,
        compiler_params=pltpu.CompilerParams(vmem_limit_bytes=40 * 2**20),
        cost_estimate=pl.CostEstimate(flops=flops, bytes_accessed=moved, transcendentals=0),
    )(*leaves, *after)


def iota(shape, axis):
    return lax.broadcasted_iota(jnp.int32, shape, axis)


def one_hot(condition):
    return jnp.where(condition, 1.0, 0.0).astype(jnp.bfloat16)


TAGS = {
    0: ((0,), ()),
    1: ((1, 3, 6, 4), ()),
    2: ((2, 5), ((1, 1), (1, 3))),
    7: ((7,), ((1, 2), (2, 1), (2, 3))),
}
TAG_LINE = ((0, 0), (1, 0), (2, 0), (2, 2), (7, 3), (7, 2), (7, 1), (7, 0))
STEPS = (((6, 4), ()), ((1, 0), ()), ((2, 5), (1,)), ((7, 3), (1, 2)))


def pack(send, blocks, unit, place, position, arrived, outs):
    rows, width = unit.shape
    if position is not None:
        parts = jnp.where(iota((16, rows), 0) == 0, position // TAG_BASE, position % TAG_BASE)
        parts = parts.astype(jnp.float32).astype(jnp.bfloat16)

    def chosen(block):
        return one_hot(iota((send, rows), 0) + block * send == place)

    def tag_line(block):
        found = dot(parts, chosen(block), ROWS_BY_ROWS)
        return jnp.concatenate([found[0:1], found[1:2]], axis=1)

    for block, out in zip(blocks, outs):
        out[:send, :] = dot(chosen(block), unit).astype(jnp.bfloat16)
        if block in TAGS:
            own, handed = TAGS[block]
            lines = [tag_line(b) for b in own]
            lines += [arrived[c][send:, : 2 * send][n : n + 1] for c, n in handed]
            lines = [line.astype(jnp.float32) for line in lines]
            lines.append(jnp.zeros((TAG_ROWS - len(lines), 2 * send), jnp.float32))
            lines = jnp.concatenate(lines, axis=0)
            rest = jnp.zeros((TAG_ROWS, width - 2 * send), jnp.float32)
            out[send:, :] = jnp.concatenate([lines, rest], axis=1).astype(jnp.bfloat16)


def unit_body(embeds_ref, unit_ref):
    values = embeds_ref[...].astype(jnp.float32)
    mean = jnp.sum(values * values, axis=1, keepdims=True) / values.shape[1]
    unit_ref[...] = (values * lax.rsqrt(mean + EPS)).astype(jnp.bfloat16)


def first_body(owners, send, blocks, unit_ref, cluster_ref, base_ref, place_ref, *outs):
    rows = cluster_ref.shape[1]
    owner = cluster_ref[...] ^ base_ref[...]
    which = iota((max(owners, 16), rows), 0) == owner
    before = one_hot(iota((rows, rows), 0) < iota((rows, rows), 1))
    counts = dot(one_hot(which), before)
    rank = jnp.sum(jnp.where(which, counts, 0.0), axis=0, keepdims=True)
    place = owner * send + rank.astype(jnp.int32)
    place_ref[...] = place
    if blocks:
        pack(send, blocks, unit_ref[...], place, None, {}, outs)
    else:
        (out,) = outs
        chosen = one_hot(iota((out.shape[0], rows), 0) == place)
        out[...] = dot(chosen, unit_ref[...]).astype(jnp.bfloat16)


def pack_body(send, blocks, unit_ref, place_ref, order_ref, arrived, *outs):
    position = order_ref[...] % HALF + 1
    pack(send, blocks, unit_ref[...], place_ref[...], position, arrived, outs)


def tags_of(chunks, tags, send):
    if tags:
        return tags[0][...]
    found = []
    for chunk, line in TAG_LINE:
        lines = chunks[chunk][send:, : 2 * send].astype(jnp.float32)[line : line + 1]
        found.append(lines[:, :send] * TAG_BASE + lines[:, send:])
    found = jnp.concatenate(found, axis=1).astype(jnp.int32)
    return jnp.where(found == 0, EMPTY, found - 1)


def rows_of(chunks, send):
    if 1 not in chunks:
        return chunks[0][...]
    return jnp.concatenate([chunks[k][:send, :] for k in range(8)], axis=0)


def border_body(send, chunks, want_ref, tags, keep_ref, give_ref):
    chosen = one_hot(want_ref[...] == tags_of(chunks, tags, send))
    picked = dot(chosen, rows_of(chunks, send)).astype(jnp.bfloat16)
    keep_ref[...] = picked[: BORDER // 2]
    give_ref[...] = picked[BORDER // 2 :]


def place_body(send, chunks, tags, *mine_refs):
    tags = tags_of(chunks, tags, send)
    rows = rows_of(chunks, send)
    first = 0
    for mine_ref in mine_refs:
        count = mine_ref.shape[0]
        chosen = one_hot(iota((count, tags.shape[1]), 0) + first == tags)
        mine_ref[...] = dot(chosen, rows).astype(jnp.bfloat16)
        first += count


def weigh(products, width):
    return jnp.exp((products / width - 1.0) / SCALE)


def near_body(mine_refs, other_refs, near_ref):
    mine = jnp.concatenate([ref[...] for ref in mine_refs], axis=0)
    other = jnp.concatenate([ref[...] for ref in other_refs], axis=0)
    width = mine.shape[1]
    own = weigh(dot(mine, mine, ROWS_BY_ROWS), width)
    own = jnp.where(iota(own.shape, 0) == iota(own.shape, 1), 0.0, own)
    across = weigh(dot(other, mine, ROWS_BY_ROWS), width)
    near_ref[...] = jnp.sum(own, axis=0, keepdims=True) + jnp.sum(across, axis=0, keepdims=True)


def far_body(mine_refs, other_refs, tile_ref, near_ref, here_ref, there_ref):
    tile = tile_ref[...]
    for rows_refs, out_ref in ((mine_refs, here_ref), (other_refs, there_ref)):
        rows = jnp.concatenate([ref[...] for ref in rows_refs], axis=0)
        far = weigh(dot(tile, rows, ROWS_BY_ROWS), tile.shape[1])
        total = jnp.sum(far, axis=0, keepdims=True)
        if out_ref is here_ref:
            total = total + near_ref[...]
        for r in range(HALF // LANES):
            out_ref[r : r + 1, :] = total[:, r * LANES : (r + 1) * LANES]


def answer_body(scores_ref, cluster_ref, order_ref, base_ref, out_ref):
    lines_each = HALF // LANES
    place = order_ref[...] % HALF
    line = (cluster_ref[...] ^ base_ref[...]) * lines_each + place // LANES
    lane = place % LANES

    def add(n, found):
        scores = jnp.broadcast_to(scores_ref[pl.ds(n, 1), :], lane.shape)
        there = jnp.take_along_axis(scores, lane, axis=1)
        return jnp.where(line == n, there, found)

    lines = scores_ref.shape[0]
    found = jnp.zeros(lane.shape, jnp.float32)
    out_ref[...] = lax.fori_loop(0, lines, add, found, unroll=lines <= 64)


def per_device(embeds, cluster_of, order_in, partner, border_idx):
    rows, width = embeds.shape
    clus_count = lax.axis_size("clus")
    owners = clus_count * lax.axis_size("sub")
    send = 2 * rows // owners
    me = lax.axis_index(OWNERS)
    side = lax.axis_index("rep")
    swap = [(0, 1), (1, 0)]
    paired = owners == 8

    def toward(x, flip):
        return lax.ppermute(x, OWNERS, [(i, i ^ flip) for i in range(owners)])

    def across(x, flip):
        pairs = [(2 * i + r, 2 * (i ^ flip) + 1 - r) for i in range(owners) for r in range(2)]
        return lax.ppermute(x, (*OWNERS, "rep"), pairs)

    def gather(x):
        return lax.all_gather(x, OWNERS, axis=0, tiled=True)

    def gather_halves(mine, other):
        if not paired:
            return gather(mine)
        for flip in (1, 2, 4):
            arrived = across(jnp.concatenate([other, mine]) if flip < 4 else other, flip)
            mine = jnp.concatenate([mine, arrived[: mine.shape[0]]])
            if flip < 4:
                other = jnp.concatenate([other, arrived[other.shape[0] :]])
        return mine

    base = me if paired else jnp.zeros_like(me)
    base = base.reshape(1, 1)
    cluster_row = cluster_of.reshape(1, rows)
    order_row = order_in.reshape(1, rows)

    def shapes(blocks):
        sizes = [(send + TAG_ROWS * (b in TAGS), width) for b in blocks] or [(owners * send, width)]
        return [jax.ShapeDtypeStruct(size, jnp.bfloat16) for size in sizes]

    unit = call(unit_body, jax.ShapeDtypeStruct((rows, width), jnp.bfloat16), 0, embeds)

    def first(blocks):
        return call(
            functools.partial(first_body, owners, send, blocks),
            [jax.ShapeDtypeStruct((1, rows), jnp.int32), *shapes(blocks)],
            2 * rows * rows * width,
            unit,
            cluster_row,
            base,
        )

    if paired:
        chunks = {}
        for blocks, needed in STEPS:
            if not chunks:
                place, *packed = first(blocks)
            else:
                handed = {k: chunks[k] for k in needed}
                packed = call(
                    functools.partial(pack_body, send, blocks),
                    shapes(blocks),
                    2 * len(blocks) * send * rows * width,
                    unit,
                    place,
                    order_row,
                    handed,
                )
            for block, chunk in zip(blocks, packed):
                chunks[block] = toward(chunk, block) if block else chunk
        tags = []
    else:
        _, blocks = first(())
        blocks = blocks.reshape(owners, send, width)
        blocks = lax.all_to_all(blocks, OWNERS, split_axis=0, concat_axis=0, tiled=True)
        chunks = {0: blocks.reshape(owners * send, width)}
        every = gather(cluster_of * CAP + order_in).reshape(owners, rows)
        mask = (every // CAP) == me
        index = jnp.arange(rows, dtype=jnp.int32)
        before = (index[:, None] < index[None, :]).astype(jnp.bfloat16)
        rank = dot(mask.astype(jnp.bfloat16), before).astype(jnp.int32)
        rank = jnp.where(mask, rank, -1)
        hit = rank[:, None, :] == index[None, :send, None]
        found = jnp.sum(jnp.where(hit, (every % HALF - EMPTY)[:, None, :], 0), axis=2) + EMPTY
        tags = [found.reshape(1, owners * send)]

    want = border_idx.reshape(BORDER, 1) - side * HALF
    want = jnp.where(side == 0, want, jnp.roll(want, BORDER // 2, axis=0))
    by = clus_count // 2
    opposite = [
        (2 * i + r, 2 * ((i + by) % clus_count) + 1 - r) for i in range(clus_count) for r in range(2)
    ]
    part = jax.ShapeDtypeStruct((BORDER // 2, width), jnp.bfloat16)
    keep, give = call(
        functools.partial(border_body, send),
        [part, part],
        2 * BORDER * owners * send * width,
        chunks,
        want,
        tags,
    )
    tile = lax.ppermute(keep + lax.ppermute(give, "rep", swap), ("clus", "rep"), opposite)
    part = jax.ShapeDtypeStruct((HALF // PIECES, width), jnp.bfloat16)
    mine = call(
        functools.partial(place_body, send),
        [part] * PIECES,
        2 * HALF * owners * send * width,
        chunks,
        tags,
        after=[give],
    )
    other = [lax.ppermute(part, "rep", swap) for part in mine]
    near = call(
        near_body,
        jax.ShapeDtypeStruct((1, HALF), jnp.float32),
        2 * HALF * CAP * width,
        mine,
        other,
    )
    lines = jax.ShapeDtypeStruct((HALF // LANES, LANES), jnp.float32)
    here, there = call(
        far_body,
        [lines, lines],
        2 * HALF * BORDER * width,
        mine,
        other,
        tile,
        near,
    )
    swapped = lax.ppermute(jnp.concatenate([there, here]), "rep", swap)
    totals = jnp.concatenate([here, there]) + swapped
    scores = -jnp.log(totals / (CAP - 1 + BORDER))
    lines = HALF // LANES
    answers = call(
        answer_body,
        jax.ShapeDtypeStruct((rows // LANES, LANES), jnp.float32),
        owners * HALF,
        gather_halves(scores[:lines], scores[lines:]),
        cluster_of.reshape(rows // LANES, LANES),
        order_in.reshape(rows // LANES, LANES),
        base,
    )
    return answers.reshape(rows)


def solution(mesh):
    return jax.shard_map(
        per_device,
        mesh=mesh,
        in_specs=(
            P(("groups", "clus", "sub", "rep"), None),
            P(("groups", "clus", "sub", "rep")),
            P(("groups", "clus", "sub", "rep")),
            P(("groups", "clus", "sub")),
            P(("groups", "clus", "sub"), None),
        ),
        out_specs=P(("groups", "clus", "sub", "rep")),
        check_vma=False,
    )
```

```python
import functools

import jax
import jax.numpy as jnp
from jax import lax
from jax.experimental import pallas as pl
from jax.experimental.pallas import tpu as pltpu
from jax.sharding import PartitionSpec as P

CAP = 1024
HALF = CAP // 2
BORDER = 256
EPS = 1e-06
SCALE = 0.1
LANES = 128
TAG_ROWS = 8
TAG_BASE = 32
EMPTY = 4096
PIECES = (64, 112, 112, 112, 112)
OWNERS = ("clus", "sub")

ROWS_BY_ROWS = (((1,), (1,)), ((), ()))


def dot(a, b, dims=(((1,), (0,)), ((), ()))):
    return lax.dot_general(a, b, dims, preferred_element_type=jnp.float32)


def call(body, out_shape, flops, *args, after=()):
    leaves, tree = jax.tree.flatten(args)
    moved = sum(a.size * a.dtype.itemsize for a in leaves)
    moved += sum(o.size * o.dtype.itemsize for o in jax.tree.leaves(out_shape))
    spec = pl.BlockSpec(memory_space=pltpu.VMEM)
    many = isinstance(out_shape, (list, tuple))
    count = len(leaves)

    def kernel(*refs):
        body(*jax.tree.unflatten(tree, refs[:count]), *refs[count + len(after) :])

    return pl.pallas_call(
        kernel,
        out_shape=out_shape,
        in_specs=[spec] * count + [pl.BlockSpec(memory_space=pl.ANY)] * len(after),
        out_specs=[spec] * len(out_shape) if many else spec,
        compiler_params=pltpu.CompilerParams(vmem_limit_bytes=40 * 2**20),
        cost_estimate=pl.CostEstimate(
            flops=flops, bytes_accessed=moved if flops else 0, transcendentals=0
        ),
    )(*leaves, *after)


def iota(shape, axis):
    return lax.broadcasted_iota(jnp.int32, shape, axis)


def one_hot(condition):
    return jnp.where(condition, 1.0, 0.0).astype(jnp.bfloat16)


TAGS = {
    0: ((0,), ()),
    1: ((1, 3, 6, 4), ()),
    2: ((2, 5), ((1, 1), (1, 3))),
    7: ((7,), ((1, 2), (2, 1), (2, 3))),
}
TAG_LINE = ((0, 0), (1, 0), (2, 0), (2, 2), (7, 3), (7, 2), (7, 1), (7, 0))
STEPS = (((6, 4), ()), ((1, 0), ()), ((2, 5), (1,)), ((7, 3), (1, 2)))


def pack(send, blocks, unit, place, position, arrived, outs):
    rows, width = unit.shape
    if position is not None:
        parts = jnp.where(iota((16, rows), 0) == 0, position // TAG_BASE, position % TAG_BASE)
        parts = parts.astype(jnp.float32).astype(jnp.bfloat16)

    def chosen(block):
        return one_hot(iota((send, rows), 0) + block * send == place)

    def tag_line(block):
        found = dot(parts, chosen(block), ROWS_BY_ROWS)
        return jnp.concatenate([found[0:1], found[1:2]], axis=1)

    for block, out in zip(blocks, outs):
        out[:send, :] = dot(chosen(block), unit).astype(jnp.bfloat16)
        if block in TAGS:
            own, handed = TAGS[block]
            lines = [tag_line(b) for b in own]
            lines += [arrived[c][send:, : 2 * send][n : n + 1] for c, n in handed]
            lines = [line.astype(jnp.float32) for line in lines]
            lines.append(jnp.zeros((TAG_ROWS - len(lines), 2 * send), jnp.float32))
            lines = jnp.concatenate(lines, axis=0)
            rest = jnp.zeros((TAG_ROWS, width - 2 * send), jnp.float32)
            out[send:, :] = jnp.concatenate([lines, rest], axis=1).astype(jnp.bfloat16)


def unit_body(embeds_ref, unit_ref):
    values = embeds_ref[...].astype(jnp.float32)
    mean = jnp.sum(values * values, axis=1, keepdims=True) / values.shape[1]
    unit_ref[...] = (values * lax.rsqrt(mean + EPS)).astype(jnp.bfloat16)


def first_body(owners, send, blocks, unit_ref, cluster_ref, base_ref, place_ref, *outs):
    rows = cluster_ref.shape[1]
    owner = cluster_ref[...] ^ base_ref[...]
    which = iota((max(owners, 16), rows), 0) == owner
    before = one_hot(iota((rows, rows), 0) < iota((rows, rows), 1))
    counts = dot(one_hot(which), before)
    rank = jnp.sum(jnp.where(which, counts, 0.0), axis=0, keepdims=True)
    place = owner * send + rank.astype(jnp.int32)
    place_ref[...] = place
    if blocks:
        pack(send, blocks, unit_ref[...], place, None, {}, outs)
    else:
        (out,) = outs
        chosen = one_hot(iota((out.shape[0], rows), 0) == place)
        out[...] = dot(chosen, unit_ref[...]).astype(jnp.bfloat16)


def pack_body(send, blocks, unit_ref, place_ref, order_ref, arrived, *outs):
    position = order_ref[...] % HALF + 1
    pack(send, blocks, unit_ref[...], place_ref[...], position, arrived, outs)


def tags_of(chunks, tags, send):
    if tags:
        return tags[0][...]
    found = []
    for chunk, line in TAG_LINE:
        lines = chunks[chunk][send:, : 2 * send].astype(jnp.float32)[line : line + 1]
        found.append(lines[:, :send] * TAG_BASE + lines[:, send:])
    found = jnp.concatenate(found, axis=1).astype(jnp.int32)
    return jnp.where(found == 0, EMPTY, found - 1)


def rows_of(chunks, send):
    if 1 not in chunks:
        return chunks[0][...]
    return jnp.concatenate([chunks[k][:send, :] for k in range(8)], axis=0)


def border_body(send, chunks, want_ref, tags, keep_ref, give_ref, head_ref):
    tags = tags_of(chunks, tags, send)
    first = iota((head_ref.shape[0], tags.shape[1]), 0)
    chosen = jnp.concatenate([one_hot(want_ref[...] == tags), one_hot(first == tags)], axis=0)
    picked = dot(chosen, rows_of(chunks, send)).astype(jnp.bfloat16)
    keep_ref[...] = picked[: BORDER // 2]
    give_ref[...] = picked[BORDER // 2 : BORDER]
    head_ref[...] = picked[BORDER:]


def place_body(send, chunks, tags, *mine_refs):
    tags = tags_of(chunks, tags, send)
    first = HALF - sum(ref.shape[0] for ref in mine_refs)
    chosen = one_hot(iota((HALF - first, tags.shape[1]), 0) + first == tags)
    placed = dot(chosen, rows_of(chunks, send)).astype(jnp.bfloat16)
    first = 0
    for ref in mine_refs:
        ref[...] = placed[first : first + ref.shape[0]]
        first += ref.shape[0]


def weigh(products, width):
    return jnp.exp((products / width - 1.0) / SCALE)


def near_body(mine_refs, other_refs, near_ref):
    mine = jnp.concatenate([ref[...] for ref in mine_refs], axis=0)
    other = jnp.concatenate([ref[...] for ref in other_refs], axis=0)
    width = mine.shape[1]
    own = weigh(dot(mine, mine, ROWS_BY_ROWS), width)
    own = jnp.where(iota(own.shape, 0) == iota(own.shape, 1), 0.0, own)
    across = weigh(dot(other, mine, ROWS_BY_ROWS), width)
    near_ref[...] = jnp.sum(own, axis=0, keepdims=True) + jnp.sum(across, axis=0, keepdims=True)


def far_body(mine_refs, other_refs, tile_ref, near_ref, here_ref, there_ref):
    tile = tile_ref[...]
    for rows_refs, out_ref in ((mine_refs, here_ref), (other_refs, there_ref)):
        rows = jnp.concatenate([ref[...] for ref in rows_refs], axis=0)
        far = weigh(dot(tile, rows, ROWS_BY_ROWS), tile.shape[1])
        total = jnp.sum(far, axis=0, keepdims=True)
        if out_ref is here_ref:
            total = total + near_ref[...]
        for r in range(HALF // LANES):
            out_ref[r : r + 1, :] = total[:, r * LANES : (r + 1) * LANES]


def answer_body(scores_ref, cluster_ref, order_ref, base_ref, out_ref):
    lines_each = HALF // LANES
    place = order_ref[...] % HALF
    line = (cluster_ref[...] ^ base_ref[...]) * lines_each + place // LANES
    lane = place % LANES

    def add(n, found):
        scores = jnp.broadcast_to(scores_ref[pl.ds(n, 1), :], lane.shape)
        there = jnp.take_along_axis(scores, lane, axis=1)
        return jnp.where(line == n, there, found)

    lines = scores_ref.shape[0]
    found = jnp.zeros(lane.shape, jnp.float32)
    out_ref[...] = lax.fori_loop(0, lines, add, found, unroll=lines <= 64)


def per_device(embeds, cluster_of, order_in, partner, border_idx):
    rows, width = embeds.shape
    clus_count = lax.axis_size("clus")
    owners = clus_count * lax.axis_size("sub")
    send = 2 * rows // owners
    me = lax.axis_index(OWNERS)
    side = lax.axis_index("rep")
    swap = [(0, 1), (1, 0)]
    paired = owners == 8

    def toward(x, flip):
        return lax.ppermute(x, OWNERS, [(i, i ^ flip) for i in range(owners)])

    def across(x, flip):
        pairs = [(2 * i + r, 2 * (i ^ flip) + 1 - r) for i in range(owners) for r in range(2)]
        return lax.ppermute(x, (*OWNERS, "rep"), pairs)

    def gather(x):
        return lax.all_gather(x, OWNERS, axis=0, tiled=True)

    def gather_halves(mine, other):
        if not paired:
            return gather(mine)
        for flip in (1, 2, 4):
            arrived = across(jnp.concatenate([other, mine]) if flip < 4 else other, flip)
            mine = jnp.concatenate([mine, arrived[: mine.shape[0]]])
            if flip < 4:
                other = jnp.concatenate([other, arrived[other.shape[0] :]])
        return mine

    base = me if paired else jnp.zeros_like(me)
    base = base.reshape(1, 1)
    cluster_row = cluster_of.reshape(1, rows)
    order_row = order_in.reshape(1, rows)

    def shapes(blocks):
        sizes = [(send + TAG_ROWS * (b in TAGS), width) for b in blocks] or [(owners * send, width)]
        return [jax.ShapeDtypeStruct(size, jnp.bfloat16) for size in sizes]

    unit = call(unit_body, jax.ShapeDtypeStruct((rows, width), jnp.bfloat16), 0, embeds)

    def first(blocks):
        return call(
            functools.partial(first_body, owners, send, blocks),
            [jax.ShapeDtypeStruct((1, rows), jnp.int32), *shapes(blocks)],
            2 * rows * rows * width,
            unit,
            cluster_row,
            base,
        )

    if paired:
        chunks = {}
        for blocks, needed in STEPS:
            if not chunks:
                place, *packed = first(blocks)
            else:
                handed = {k: chunks[k] for k in needed}
                packed = call(
                    functools.partial(pack_body, send, blocks),
                    shapes(blocks),
                    2 * len(blocks) * send * rows * width,
                    unit,
                    place,
                    order_row,
                    handed,
                )
            for block, chunk in zip(blocks, packed):
                chunks[block] = toward(chunk, block) if block else chunk
        tags = []
    else:
        _, blocks = first(())
        blocks = blocks.reshape(owners, send, width)
        blocks = lax.all_to_all(blocks, OWNERS, split_axis=0, concat_axis=0, tiled=True)
        chunks = {0: blocks.reshape(owners * send, width)}
        every = gather(cluster_of * CAP + order_in).reshape(owners, rows)
        mask = (every // CAP) == me
        index = jnp.arange(rows, dtype=jnp.int32)
        before = (index[:, None] < index[None, :]).astype(jnp.bfloat16)
        rank = dot(mask.astype(jnp.bfloat16), before).astype(jnp.int32)
        rank = jnp.where(mask, rank, -1)
        hit = rank[:, None, :] == index[None, :send, None]
        found = jnp.sum(jnp.where(hit, (every % HALF - EMPTY)[:, None, :], 0), axis=2) + EMPTY
        tags = [found.reshape(1, owners * send)]

    want = border_idx.reshape(BORDER, 1) - side * HALF
    want = jnp.where(side == 0, want, jnp.roll(want, BORDER // 2, axis=0))
    by = clus_count // 2
    opposite = [
        (2 * i + r, 2 * ((i + by) % clus_count) + 1 - r) for i in range(clus_count) for r in range(2)
    ]
    part = jax.ShapeDtypeStruct((BORDER // 2, width), jnp.bfloat16)
    pieces = [jax.ShapeDtypeStruct((count, width), jnp.bfloat16) for count in PIECES]
    keep, give, head = call(
        functools.partial(border_body, send),
        [part, part, pieces[0]],
        2 * BORDER * owners * send * width,
        chunks,
        want,
        tags,
    )
    chosen = keep + lax.ppermute(give, "rep", swap)
    tile = lax.ppermute(chosen, ("clus", "rep"), opposite)
    rest = call(
        functools.partial(place_body, send),
        pieces[1:],
        2 * HALF * owners * send * width,
        chunks,
        tags,
        after=[give],
    )
    mine = [head, *rest]
    other = [lax.ppermute(part, "rep", swap) for part in mine]
    near = call(
        near_body,
        jax.ShapeDtypeStruct((1, HALF), jnp.float32),
        0,
        mine,
        other,
    )
    lines = jax.ShapeDtypeStruct((HALF // LANES, LANES), jnp.float32)
    here, there = call(
        far_body,
        [lines, lines],
        2 * HALF * BORDER * width,
        mine,
        other,
        tile,
        near,
    )
    swapped = lax.ppermute(jnp.concatenate([there, here]), "rep", swap)
    totals = jnp.concatenate([here, there]) + swapped
    scores = -jnp.log(totals / (CAP - 1 + BORDER))
    lines = HALF // LANES
    answers = call(
        answer_body,
        jax.ShapeDtypeStruct((rows // LANES, LANES), jnp.float32),
        owners * HALF,
        gather_halves(scores[:lines], scores[lines:]),
        cluster_of.reshape(rows // LANES, LANES),
        order_in.reshape(rows // LANES, LANES),
        base,
    )
    return answers.reshape(rows)


def solution(mesh):
    return jax.shard_map(
        per_device,
        mesh=mesh,
        in_specs=(
            P(("groups", "clus", "sub", "rep"), None),
            P(("groups", "clus", "sub", "rep")),
            P(("groups", "clus", "sub", "rep")),
            P(("groups", "clus", "sub")),
            P(("groups", "clus", "sub"), None),
        ),
        out_specs=P(("groups", "clus", "sub", "rep")),
        check_vma=False,
    )
```

```python
import functools
import math

import jax
import jax.numpy as jnp
from jax import lax
from jax.experimental import pallas as pl
from jax.experimental.pallas import tpu as pltpu
from jax.sharding import PartitionSpec as P

CAP = 1024
HALF = CAP // 2
BORDER = 256
EPS = 1e-06
SCALE = 0.1
LANES = 128
TAG_ROWS = 8
TAG_BASE = 32
EMPTY = 4096
PIECES = (64, 112, 112, 112, 112)
OWNERS = ("clus", "sub")

ROWS_BY_ROWS = (((1,), (1,)), ((), ()))


def dot(a, b, dims=(((1,), (0,)), ((), ()))):
    return lax.dot_general(a, b, dims, preferred_element_type=jnp.float32)


def call(body, out_shape, flops, *args, after=()):
    leaves, tree = jax.tree.flatten(args)
    moved = sum(a.size * a.dtype.itemsize for a in leaves)
    moved += sum(o.size * o.dtype.itemsize for o in jax.tree.leaves(out_shape))
    spec = pl.BlockSpec(memory_space=pltpu.VMEM)
    many = isinstance(out_shape, (list, tuple))
    count = len(leaves)

    def kernel(*refs):
        body(*jax.tree.unflatten(tree, refs[:count]), *refs[count + len(after) :])

    return pl.pallas_call(
        kernel,
        out_shape=out_shape,
        in_specs=[spec] * count + [pl.BlockSpec(memory_space=pl.ANY)] * len(after),
        out_specs=[spec] * len(out_shape) if many else spec,
        compiler_params=pltpu.CompilerParams(vmem_limit_bytes=40 * 2**20),
        cost_estimate=pl.CostEstimate(
            flops=flops, bytes_accessed=moved if flops else 0, transcendentals=0
        ),
    )(*leaves, *after)


def iota(shape, axis):
    return lax.broadcasted_iota(jnp.int32, shape, axis)


def one_hot(condition):
    return jnp.where(condition, 1.0, 0.0).astype(jnp.bfloat16)


TAGS = {
    0: ((0,), ()),
    1: ((1, 3, 6, 4), ()),
    2: ((2, 5), ((1, 1), (1, 3))),
    7: ((7,), ((1, 2), (2, 1), (2, 3))),
}
TAG_LINE = ((0, 0), (1, 0), (2, 0), (2, 2), (7, 3), (7, 2), (7, 1), (7, 0))
STEPS = (((6, 4), ()), ((1, 0), ()), ((2, 5), (1,)), ((7, 3), (1, 2)))


BELOW = {0: TAG_ROWS, 1: 6 * TAG_ROWS, 2: 6 * TAG_ROWS, 7: TAG_ROWS}


def chunk_shape(block, send, width):
    if block in TAGS:
        return width // LANES * send + BELOW[block], LANES
    return send, width


def rows_in(chunk, send):
    if chunk.shape[0] == send:
        return chunk[...]
    columns = [chunk[n : n + send, :] for n in range(0, chunk.shape[0] - send + 1, send)]
    return jnp.concatenate(columns, axis=1)


def digits_in(chunk, send):
    first = chunk.shape[0] // send * send
    return chunk[first : first + TAG_ROWS, :].astype(jnp.float32)


def pack(send, blocks, unit, place, position, arrived, outs):
    rows, width = unit.shape
    if position is not None:
        parts = jnp.where(iota((16, rows), 0) == 0, position // TAG_BASE, position % TAG_BASE)
        parts = parts.astype(jnp.float32).astype(jnp.bfloat16)
    digits = {k: digits_in(ref, send) for k, ref in arrived.items()}

    def chosen(block):
        return one_hot(iota((send, rows), 0) + block * send == place)

    for block, out in zip(blocks, outs):
        packed = dot(chosen(block), unit).astype(jnp.bfloat16)
        if block not in TAGS:
            out[...] = packed
            continue
        for n in range(width // LANES):
            out[n * send : (n + 1) * send, :] = packed[:, n * LANES : (n + 1) * LANES]
        own, handed = TAGS[block]
        lines = []
        for b in own:
            found = dot(parts, chosen(b), ROWS_BY_ROWS)
            lines.append((found[0:1], found[1:2]))
        for c, n in handed:
            lines.append((digits[c][n : n + 1], digits[c][n + TAG_ROWS // 2 :][:1]))
        lines += [(jnp.zeros((1, send), jnp.float32),) * 2] * (TAG_ROWS // 2 - len(lines))
        lines = [high for high, _ in lines] + [low for _, low in lines]
        rest = jnp.zeros((BELOW[block] - TAG_ROWS, send), jnp.float32)
        lines = jnp.concatenate([*lines, rest] if rest.size else lines, axis=0)
        out[width // LANES * send :, :] = lines.astype(jnp.bfloat16)


def steps_body(steps_ref):
    steps_ref[...] = one_hot(iota(steps_ref.shape, 0) % LANES < iota(steps_ref.shape, 1))
    steps_ref[LANES:, :] = jnp.ones((LANES, LANES), jnp.bfloat16)


def ranks(which, steps):
    lines, rows = which.shape
    hits = jnp.where(which, 1.0, 0.0)
    sums = jnp.zeros((lines, LANES), jnp.float32)
    parts, totals = [], []
    for n in range(0, rows, LANES):
        parts.append(hits[:, n : n + LANES])
        totals.append(sums)
        sums = sums + parts[-1]
    both = [jnp.concatenate(x, axis=0).astype(jnp.bfloat16) for x in (parts, totals)]
    found = dot(jnp.concatenate(both, axis=1), steps)
    return jnp.concatenate([found[n : n + lines] for n in range(0, found.shape[0], lines)], axis=1)


def place_of_body(owners, send, steps_ref, cluster_ref, base_ref, place_ref):
    owner = cluster_ref[...] ^ base_ref[...]
    which = iota((max(owners, 16), cluster_ref.shape[1]), 0) == owner
    rank = jnp.sum(jnp.where(which, ranks(which, steps_ref[...]), 0.0), axis=0, keepdims=True)
    place_ref[...] = owner * send + rank.astype(jnp.int32)


def first_body(send, blocks, embeds_ref, place_ref, unit_ref, *outs):
    values = embeds_ref[...].astype(jnp.float32)
    mean = jnp.sum(values * values, axis=1, keepdims=True) / values.shape[1]
    unit = (values * lax.rsqrt(mean + EPS)).astype(jnp.bfloat16)
    unit_ref[...] = unit
    place = place_ref[...]
    if blocks:
        pack(send, blocks, unit, place, None, {}, outs)
    else:
        (out,) = outs
        chosen = one_hot(iota((out.shape[0], place.shape[1]), 0) == place)
        out[...] = dot(chosen, unit).astype(jnp.bfloat16)


def pack_body(send, blocks, unit_ref, place_ref, order_ref, arrived, *outs):
    position = order_ref[...] % HALF + 1
    pack(send, blocks, unit_ref[...], place_ref[...], position, arrived, outs)


def tags_of(chunks, tags, send):
    if tags:
        return tags[0][...]
    digits = {k: digits_in(chunks[k], send) for k in TAGS}
    found = []
    for k, n in TAG_LINE:
        low = n + TAG_ROWS // 2
        found.append(digits[k][n : n + 1] * TAG_BASE + digits[k][low : low + 1])
    found = jnp.concatenate(found, axis=1).astype(jnp.int32)
    return jnp.where(found == 0, EMPTY, found - 1)


def rows_of(chunks, send):
    if 1 not in chunks:
        return chunks[0][...]
    return jnp.concatenate([rows_in(chunks[k], send) for k in range(8)], axis=0)


def give_body(send, chunks, want_ref, tags, give_ref):
    chosen = one_hot(want_ref[BORDER // 2 :, :] == tags_of(chunks, tags, send))
    give_ref[...] = dot(chosen, rows_of(chunks, send)).astype(jnp.bfloat16)


def keep_body(send, chunks, want_ref, tags, keep_ref, head_ref):
    tags = tags_of(chunks, tags, send)
    first = iota((head_ref.shape[0], tags.shape[1]), 0)
    chosen = [one_hot(want_ref[: BORDER // 2, :] == tags), one_hot(first == tags)]
    chosen = jnp.concatenate(chosen, axis=0)
    picked = dot(chosen, rows_of(chunks, send)).astype(jnp.bfloat16)
    keep_ref[...] = picked[: keep_ref.shape[0]]
    head_ref[...] = picked[keep_ref.shape[0] :]


def place_body(send, chunks, tags, *mine_refs):
    tags = tags_of(chunks, tags, send)
    first = HALF - sum(ref.shape[0] for ref in mine_refs)
    chosen = one_hot(iota((HALF - first, tags.shape[1]), 0) + first == tags)
    placed = dot(chosen, rows_of(chunks, send)).astype(jnp.bfloat16)
    first = 0
    for ref in mine_refs:
        ref[...] = placed[first : first + ref.shape[0]]
        first += ref.shape[0]


def weigh(products, width):
    by = math.log2(math.e) / SCALE
    return jnp.exp2(products * (by / width) - by)


def near_body(mine_refs, other_refs, near_ref):
    mine = jnp.concatenate([ref[...] for ref in mine_refs], axis=0)
    other = jnp.concatenate([ref[...] for ref in other_refs], axis=0)
    width = mine.shape[1]
    own = weigh(dot(mine, mine, ROWS_BY_ROWS), width)
    own = jnp.where(iota(own.shape, 0) == iota(own.shape, 1), 0.0, own)
    across = weigh(dot(other, mine, ROWS_BY_ROWS), width)
    near_ref[...] = jnp.sum(own, axis=0, keepdims=True) + jnp.sum(across, axis=0, keepdims=True)


def far_body(mine_refs, other_refs, tile_ref, near_ref, here_ref, there_ref):
    tile = tile_ref[...]
    for rows_refs, out_ref in ((mine_refs, here_ref), (other_refs, there_ref)):
        rows = jnp.concatenate([ref[...] for ref in rows_refs], axis=0)
        far = weigh(dot(tile, rows, ROWS_BY_ROWS), tile.shape[1])
        total = jnp.sum(far, axis=0, keepdims=True)
        if out_ref is here_ref:
            total = total + near_ref[...]
        for r in range(HALF // LANES):
            out_ref[r : r + 1, :] = total[:, r * LANES : (r + 1) * LANES]


def answer_body(scores_ref, cluster_ref, order_ref, base_ref, out_ref):
    lines_each = HALF // LANES
    place = order_ref[...] % HALF
    line = (cluster_ref[...] ^ base_ref[...]) * lines_each + place // LANES
    lane = place % LANES

    def add(n, found):
        scores = jnp.broadcast_to(scores_ref[pl.ds(n, 1), :], lane.shape)
        there = jnp.take_along_axis(scores, lane, axis=1)
        return jnp.where(line == n, there, found)

    lines = scores_ref.shape[0]
    found = jnp.zeros(lane.shape, jnp.float32)
    out_ref[...] = lax.fori_loop(0, lines, add, found, unroll=lines <= 64)


def per_device(embeds, cluster_of, order_in, partner, border_idx):
    rows, width = embeds.shape
    clus_count = lax.axis_size("clus")
    owners = clus_count * lax.axis_size("sub")
    send = 2 * rows // owners
    me = lax.axis_index(OWNERS)
    side = lax.axis_index("rep")
    swap = [(0, 1), (1, 0)]
    paired = owners == 8

    def toward(x, flip):
        return lax.ppermute(x, OWNERS, [(i, i ^ flip) for i in range(owners)])

    def across(x, flip):
        pairs = [(2 * i + r, 2 * (i ^ flip) + 1 - r) for i in range(owners) for r in range(2)]
        return lax.ppermute(x, (*OWNERS, "rep"), pairs)

    def gather(x):
        return lax.all_gather(x, OWNERS, axis=0, tiled=True)

    def gather_halves(mine, other):
        if not paired:
            return gather(mine)
        for flip in (1, 2, 4):
            arrived = across(jnp.concatenate([other, mine]) if flip < 4 else other, flip)
            mine = jnp.concatenate([mine, arrived[: mine.shape[0]]])
            if flip < 4:
                other = jnp.concatenate([other, arrived[other.shape[0] :]])
        return mine

    base = me if paired else jnp.zeros_like(me)
    base = base.reshape(1, 1)
    cluster_row = cluster_of.reshape(1, rows)
    order_row = order_in.reshape(1, rows)

    def shapes(blocks):
        sizes = [chunk_shape(b, send, width) for b in blocks] or [(owners * send, width)]
        return [jax.ShapeDtypeStruct(size, jnp.bfloat16) for size in sizes]

    steps = call(steps_body, jax.ShapeDtypeStruct((2 * LANES, LANES), jnp.bfloat16), 2 * 10**9)
    place = call(
        functools.partial(place_of_body, owners, send),
        jax.ShapeDtypeStruct((1, rows), jnp.int32),
        10**8,
        steps,
        cluster_row,
        base,
    )

    def first(blocks):
        return call(
            functools.partial(first_body, send, blocks),
            [jax.ShapeDtypeStruct((rows, width), jnp.bfloat16), *shapes(blocks)],
            2 * rows * rows * width,
            embeds,
            place,
        )

    if paired:
        chunks = {}
        for blocks, needed in STEPS:
            if not chunks:
                unit, *packed = first(blocks)
            else:
                handed = {k: chunks[k] for k in needed}
                packed = call(
                    functools.partial(pack_body, send, blocks),
                    shapes(blocks),
                    2 * len(blocks) * send * rows * width,
                    unit,
                    place,
                    order_row,
                    handed,
                )
            for block, chunk in zip(blocks, packed):
                chunks[block] = toward(chunk, block) if block else chunk
        tags = []
    else:
        _, blocks = first(())
        blocks = blocks.reshape(owners, send, width)
        blocks = lax.all_to_all(blocks, OWNERS, split_axis=0, concat_axis=0, tiled=True)
        chunks = {0: blocks.reshape(owners * send, width)}
        every = gather(cluster_of * CAP + order_in).reshape(owners, rows)
        mask = (every // CAP) == me
        index = jnp.arange(rows, dtype=jnp.int32)
        before = (index[:, None] < index[None, :]).astype(jnp.bfloat16)
        rank = dot(mask.astype(jnp.bfloat16), before).astype(jnp.int32)
        rank = jnp.where(mask, rank, -1)
        hit = rank[:, None, :] == index[None, :send, None]
        found = jnp.sum(jnp.where(hit, (every % HALF - EMPTY)[:, None, :], 0), axis=2) + EMPTY
        tags = [found.reshape(1, owners * send)]

    by = clus_count // 2
    opposite = [
        (2 * i + r, 2 * ((i + by) % clus_count) + 1 - r) for i in range(clus_count) for r in range(2)
    ]
    want = border_idx.reshape(BORDER, 1) - side * HALF
    want = jnp.where(side == 0, want, jnp.roll(want, BORDER // 2, axis=0))
    part = jax.ShapeDtypeStruct((BORDER // 2, width), jnp.bfloat16)
    pieces = [jax.ShapeDtypeStruct((count, width), jnp.bfloat16) for count in PIECES]
    give = call(
        functools.partial(give_body, send),
        part,
        BORDER * owners * send * width,
        chunks,
        want,
        tags,
    )
    keep, head = call(
        functools.partial(keep_body, send),
        [part, pieces[0]],
        BORDER * owners * send * width,
        chunks,
        want,
        tags,
        after=[give],
    )
    chosen = keep + lax.ppermute(give, "rep", swap)
    tile = lax.ppermute(chosen, ("clus", "rep"), opposite)
    rest = call(
        functools.partial(place_body, send),
        pieces[1:],
        2 * HALF * owners * send * width,
        chunks,
        tags,
        after=[keep],
    )
    mine = [head, *rest]
    other = [lax.ppermute(part, "rep", swap) for part in mine]
    near = call(
        near_body,
        jax.ShapeDtypeStruct((1, HALF), jnp.float32),
        0,
        mine,
        other,
    )
    lines = jax.ShapeDtypeStruct((HALF // LANES, LANES), jnp.float32)
    here, there = call(
        far_body,
        [lines, lines],
        2 * HALF * BORDER * width,
        mine,
        other,
        tile,
        near,
    )
    swapped = lax.ppermute(jnp.concatenate([there, here]), "rep", swap)
    totals = jnp.concatenate([here, there]) + swapped
    scores = -jnp.log(totals / (CAP - 1 + BORDER))
    lines = HALF // LANES
    answers = call(
        answer_body,
        jax.ShapeDtypeStruct((rows // LANES, LANES), jnp.float32),
        owners * HALF,
        gather_halves(scores[:lines], scores[lines:]),
        cluster_of.reshape(rows // LANES, LANES),
        order_in.reshape(rows // LANES, LANES),
        base,
    )
    return answers.reshape(rows)


def solution(mesh):
    return jax.shard_map(
        per_device,
        mesh=mesh,
        in_specs=(
            P(("groups", "clus", "sub", "rep"), None),
            P(("groups", "clus", "sub", "rep")),
            P(("groups", "clus", "sub", "rep")),
            P(("groups", "clus", "sub")),
            P(("groups", "clus", "sub"), None),
        ),
        out_specs=P(("groups", "clus", "sub", "rep")),
        check_vma=False,
    )
```

```python
import functools
import math

import jax
import jax.numpy as jnp
from jax import lax
from jax.experimental import pallas as pl
from jax.experimental.pallas import tpu as pltpu
from jax.sharding import PartitionSpec as P

CAP = 1024
HALF = CAP // 2
BORDER = 256
EPS = 1e-06
SCALE = 0.1
LANES = 128
TAG_ROWS = 8
TAG_BASE = 32
EMPTY = 4096
PIECES = (64, 112, 112, 112, 112)
OWNERS = ("clus", "sub")

ROWS_BY_ROWS = (((1,), (1,)), ((), ()))


def dot(a, b, dims=(((1,), (0,)), ((), ()))):
    return lax.dot_general(a, b, dims, preferred_element_type=jnp.float32)


def call(body, out_shape, flops, *args, after=()):
    leaves, tree = jax.tree.flatten(args)
    moved = sum(a.size * a.dtype.itemsize for a in leaves)
    moved += sum(o.size * o.dtype.itemsize for o in jax.tree.leaves(out_shape))
    spec = pl.BlockSpec(memory_space=pltpu.VMEM)
    many = isinstance(out_shape, (list, tuple))
    count = len(leaves)

    def kernel(*refs):
        body(*jax.tree.unflatten(tree, refs[:count]), *refs[count + len(after) :])

    return pl.pallas_call(
        kernel,
        out_shape=out_shape,
        in_specs=[spec] * count + [pl.BlockSpec(memory_space=pl.ANY)] * len(after),
        out_specs=[spec] * len(out_shape) if many else spec,
        compiler_params=pltpu.CompilerParams(vmem_limit_bytes=40 * 2**20),
        cost_estimate=pl.CostEstimate(
            flops=flops, bytes_accessed=moved if flops else 0, transcendentals=0
        ),
    )(*leaves, *after)


def iota(shape, axis):
    return lax.broadcasted_iota(jnp.int32, shape, axis)


def one_hot(condition):
    return jnp.where(condition, 1.0, 0.0).astype(jnp.bfloat16)


TAGS = {
    0: ((0,), ()),
    1: ((1, 3, 7, 5), ()),
    2: ((2, 4), ((1, 1), (1, 3))),
    6: ((6,), ((1, 2), (2, 1), (2, 3))),
}
TAG_LINE = ((0, 0), (1, 0), (2, 0), (2, 2), (6, 2), (6, 3), (6, 0), (6, 1))
STEPS = (((7, 4), ()), ((1, 0), ()), ((2, 5), (1,)), ((6, 3), (1, 2)))


BELOW = {0: TAG_ROWS, 1: 6 * TAG_ROWS, 2: 6 * TAG_ROWS, 6: TAG_ROWS}


def chunk_shape(block, send, width):
    if block in TAGS:
        return width // LANES * send + BELOW[block], LANES
    return send, width


def rows_in(chunk, send):
    if chunk.shape[0] == send:
        return chunk[...]
    columns = [chunk[n : n + send, :] for n in range(0, chunk.shape[0] - send + 1, send)]
    return jnp.concatenate(columns, axis=1)


def digits_in(chunk, send):
    first = chunk.shape[0] // send * send
    return chunk[first : first + TAG_ROWS, :].astype(jnp.float32)


def pack(send, blocks, unit, place, position, arrived, outs):
    rows, width = unit.shape
    if position is not None:
        parts = jnp.where(iota((16, rows), 0) == 0, position // TAG_BASE, position % TAG_BASE)
        parts = parts.astype(jnp.float32).astype(jnp.bfloat16)
    digits = {k: digits_in(ref, send) for k, ref in arrived.items()}

    def chosen(block):
        return one_hot(iota((send, rows), 0) + block * send == place)

    for block, out in zip(blocks, outs):
        packed = dot(chosen(block), unit).astype(jnp.bfloat16)
        if block not in TAGS:
            out[...] = packed
            continue
        for n in range(width // LANES):
            out[n * send : (n + 1) * send, :] = packed[:, n * LANES : (n + 1) * LANES]
        own, handed = TAGS[block]
        lines = []
        for b in own:
            found = dot(parts, chosen(b), ROWS_BY_ROWS)
            lines.append((found[0:1], found[1:2]))
        for c, n in handed:
            lines.append((digits[c][n : n + 1], digits[c][n + TAG_ROWS // 2 :][:1]))
        lines += [(jnp.zeros((1, send), jnp.float32),) * 2] * (TAG_ROWS // 2 - len(lines))
        lines = [high for high, _ in lines] + [low for _, low in lines]
        rest = jnp.zeros((BELOW[block] - TAG_ROWS, send), jnp.float32)
        lines = jnp.concatenate([*lines, rest] if rest.size else lines, axis=0)
        out[width // LANES * send :, :] = lines.astype(jnp.bfloat16)


def steps_body(steps_ref):
    steps_ref[...] = one_hot(iota(steps_ref.shape, 0) % LANES < iota(steps_ref.shape, 1))
    steps_ref[LANES:, :] = jnp.ones((LANES, LANES), jnp.bfloat16)


def ranks(which, steps):
    lines, rows = which.shape
    hits = jnp.where(which, 1.0, 0.0)
    sums = jnp.zeros((lines, LANES), jnp.float32)
    parts, totals = [], []
    for n in range(0, rows, LANES):
        parts.append(hits[:, n : n + LANES])
        totals.append(sums)
        sums = sums + parts[-1]
    both = [jnp.concatenate(x, axis=0).astype(jnp.bfloat16) for x in (parts, totals)]
    found = dot(jnp.concatenate(both, axis=1), steps)
    return jnp.concatenate([found[n : n + lines] for n in range(0, found.shape[0], lines)], axis=1)


def place_of_body(owners, send, steps_ref, cluster_ref, base_ref, place_ref):
    owner = cluster_ref[...] ^ base_ref[...]
    which = iota((max(owners, 16), cluster_ref.shape[1]), 0) == owner
    rank = jnp.sum(jnp.where(which, ranks(which, steps_ref[...]), 0.0), axis=0, keepdims=True)
    place_ref[...] = owner * send + rank.astype(jnp.int32)


def first_body(send, blocks, embeds_ref, place_ref, unit_ref, *outs):
    values = embeds_ref[...].astype(jnp.float32)
    mean = jnp.sum(values * values, axis=1, keepdims=True) / values.shape[1]
    unit = (values * lax.rsqrt(mean + EPS)).astype(jnp.bfloat16)
    unit_ref[...] = unit
    place = place_ref[...]
    if blocks:
        pack(send, blocks, unit, place, None, {}, outs)
    else:
        (out,) = outs
        chosen = one_hot(iota((out.shape[0], place.shape[1]), 0) == place)
        out[...] = dot(chosen, unit).astype(jnp.bfloat16)


def pack_body(send, blocks, unit_ref, place_ref, order_ref, arrived, *outs):
    position = order_ref[...] % HALF + 1
    pack(send, blocks, unit_ref[...], place_ref[...], position, arrived, outs)


def tags_of(chunks, tags, send):
    if tags:
        return tags[0][...]
    digits = {k: digits_in(chunks[k], send) for k in TAGS}
    found = []
    for k, n in TAG_LINE:
        low = n + TAG_ROWS // 2
        found.append(digits[k][n : n + 1] * TAG_BASE + digits[k][low : low + 1])
    found = jnp.concatenate(found, axis=1).astype(jnp.int32)
    return jnp.where(found == 0, EMPTY, found - 1)


def rows_of(chunks, send):
    if 1 not in chunks:
        return chunks[0][...]
    return jnp.concatenate([rows_in(chunks[k], send) for k in range(8)], axis=0)


def give_body(send, chunks, want_ref, tags, give_ref):
    chosen = one_hot(want_ref[BORDER // 2 :, :] == tags_of(chunks, tags, send))
    give_ref[...] = dot(chosen, rows_of(chunks, send)).astype(jnp.bfloat16)


def keep_body(send, chunks, want_ref, tags, keep_ref, head_ref):
    tags = tags_of(chunks, tags, send)
    first = iota((head_ref.shape[0], tags.shape[1]), 0)
    chosen = [one_hot(want_ref[: BORDER // 2, :] == tags), one_hot(first == tags)]
    chosen = jnp.concatenate(chosen, axis=0)
    picked = dot(chosen, rows_of(chunks, send)).astype(jnp.bfloat16)
    keep_ref[...] = picked[: keep_ref.shape[0]]
    head_ref[...] = picked[keep_ref.shape[0] :]


def place_body(send, chunks, tags, *mine_refs):
    tags = tags_of(chunks, tags, send)
    first = HALF - sum(ref.shape[0] for ref in mine_refs)
    chosen = one_hot(iota((HALF - first, tags.shape[1]), 0) + first == tags)
    placed = dot(chosen, rows_of(chunks, send)).astype(jnp.bfloat16)
    first = 0
    for ref in mine_refs:
        ref[...] = placed[first : first + ref.shape[0]]
        first += ref.shape[0]


def weigh(products, width):
    by = math.log2(math.e) / SCALE
    return jnp.exp2(products * (by / width) - by)


def near_body(mine_refs, other_refs, near_ref):
    mine = jnp.concatenate([ref[...] for ref in mine_refs], axis=0)
    other = jnp.concatenate([ref[...] for ref in other_refs], axis=0)
    width = mine.shape[1]
    own = weigh(dot(mine, mine, ROWS_BY_ROWS), width)
    own = jnp.where(iota(own.shape, 0) == iota(own.shape, 1), 0.0, own)
    across = weigh(dot(other, mine, ROWS_BY_ROWS), width)
    near_ref[...] = jnp.sum(own, axis=0, keepdims=True) + jnp.sum(across, axis=0, keepdims=True)


def far_body(mine_refs, other_refs, tile_ref, near_ref, here_ref, there_ref):
    tile = tile_ref[...]
    for rows_refs, out_ref in ((mine_refs, here_ref), (other_refs, there_ref)):
        rows = jnp.concatenate([ref[...] for ref in rows_refs], axis=0)
        far = weigh(dot(tile, rows, ROWS_BY_ROWS), tile.shape[1])
        total = jnp.sum(far, axis=0, keepdims=True)
        if out_ref is here_ref:
            total = total + near_ref[...]
        for r in range(HALF // LANES):
            out_ref[r : r + 1, :] = total[:, r * LANES : (r + 1) * LANES]


def answer_body(scores_ref, cluster_ref, order_ref, base_ref, out_ref):
    lines_each = HALF // LANES
    place = order_ref[...] % HALF
    line = (cluster_ref[...] ^ base_ref[...]) * lines_each + place // LANES
    lane = place % LANES

    def add(n, found):
        scores = jnp.broadcast_to(scores_ref[pl.ds(n, 1), :], lane.shape)
        there = jnp.take_along_axis(scores, lane, axis=1)
        return jnp.where(line == n, there, found)

    lines = scores_ref.shape[0]
    found = jnp.zeros(lane.shape, jnp.float32)
    out_ref[...] = lax.fori_loop(0, lines, add, found, unroll=lines <= 64)


def per_device(embeds, cluster_of, order_in, partner, border_idx):
    rows, width = embeds.shape
    clus_count = lax.axis_size("clus")
    owners = clus_count * lax.axis_size("sub")
    send = 2 * rows // owners
    me = lax.axis_index(OWNERS)
    side = lax.axis_index("rep")
    swap = [(0, 1), (1, 0)]
    paired = owners == 8

    def toward(x, flip):
        return lax.ppermute(x, OWNERS, [(i, i ^ flip) for i in range(owners)])

    def across(x, flip):
        pairs = [(2 * i + r, 2 * (i ^ flip) + 1 - r) for i in range(owners) for r in range(2)]
        return lax.ppermute(x, (*OWNERS, "rep"), pairs)

    def gather(x):
        return lax.all_gather(x, OWNERS, axis=0, tiled=True)

    def gather_halves(mine, other):
        if not paired:
            return gather(mine)
        for flip in (1, 2, 4):
            arrived = across(jnp.concatenate([other, mine]) if flip < 4 else other, flip)
            mine = jnp.concatenate([mine, arrived[: mine.shape[0]]])
            if flip < 4:
                other = jnp.concatenate([other, arrived[other.shape[0] :]])
        return mine

    base = me if paired else jnp.zeros_like(me)
    base = base.reshape(1, 1)
    cluster_row = cluster_of.reshape(1, rows)
    order_row = order_in.reshape(1, rows)

    def shapes(blocks):
        sizes = [chunk_shape(b, send, width) for b in blocks] or [(owners * send, width)]
        return [jax.ShapeDtypeStruct(size, jnp.bfloat16) for size in sizes]

    steps = call(steps_body, jax.ShapeDtypeStruct((2 * LANES, LANES), jnp.bfloat16), 2 * 10**9)
    place = call(
        functools.partial(place_of_body, owners, send),
        jax.ShapeDtypeStruct((1, rows), jnp.int32),
        10**8,
        steps,
        cluster_row,
        base,
    )

    def first(blocks):
        return call(
            functools.partial(first_body, send, blocks),
            [jax.ShapeDtypeStruct((rows, width), jnp.bfloat16), *shapes(blocks)],
            2 * rows * rows * width,
            embeds,
            place,
        )

    if paired:
        chunks = {}
        for blocks, needed in STEPS:
            if not chunks:
                unit, *packed = first(blocks)
            else:
                handed = {k: chunks[k] for k in needed}
                packed = call(
                    functools.partial(pack_body, send, blocks),
                    shapes(blocks),
                    2 * len(blocks) * send * rows * width,
                    unit,
                    place,
                    order_row,
                    handed,
                )
            for block, chunk in zip(blocks, packed):
                chunks[block] = toward(chunk, block) if block else chunk
        tags = []
    else:
        _, blocks = first(())
        blocks = blocks.reshape(owners, send, width)
        blocks = lax.all_to_all(blocks, OWNERS, split_axis=0, concat_axis=0, tiled=True)
        chunks = {0: blocks.reshape(owners * send, width)}
        every = gather(cluster_of * CAP + order_in).reshape(owners, rows)
        mask = (every // CAP) == me
        index = jnp.arange(rows, dtype=jnp.int32)
        before = (index[:, None] < index[None, :]).astype(jnp.bfloat16)
        rank = dot(mask.astype(jnp.bfloat16), before).astype(jnp.int32)
        rank = jnp.where(mask, rank, -1)
        hit = rank[:, None, :] == index[None, :send, None]
        found = jnp.sum(jnp.where(hit, (every % HALF - EMPTY)[:, None, :], 0), axis=2) + EMPTY
        tags = [found.reshape(1, owners * send)]

    by = clus_count // 2
    opposite = [
        (2 * i + r, 2 * ((i + by) % clus_count) + 1 - r) for i in range(clus_count) for r in range(2)
    ]
    want = border_idx.reshape(BORDER, 1) - side * HALF
    want = jnp.where(side == 0, want, jnp.roll(want, BORDER // 2, axis=0))
    part = jax.ShapeDtypeStruct((BORDER // 2, width), jnp.bfloat16)
    pieces = [jax.ShapeDtypeStruct((count, width), jnp.bfloat16) for count in PIECES]
    give = call(
        functools.partial(give_body, send),
        part,
        BORDER * owners * send * width,
        chunks,
        want,
        tags,
    )
    keep, head = call(
        functools.partial(keep_body, send),
        [part, pieces[0]],
        BORDER * owners * send * width,
        chunks,
        want,
        tags,
        after=[give],
    )
    chosen = keep + lax.ppermute(give, "rep", swap)
    tile = lax.ppermute(chosen, ("clus", "rep"), opposite)
    rest = call(
        functools.partial(place_body, send),
        pieces[1:],
        2 * HALF * owners * send * width,
        chunks,
        tags,
        after=[keep],
    )
    mine = [head, *rest]
    other = [lax.ppermute(part, "rep", swap) for part in mine]
    near = call(
        near_body,
        jax.ShapeDtypeStruct((1, HALF), jnp.float32),
        0,
        mine,
        other,
    )
    lines = jax.ShapeDtypeStruct((HALF // LANES, LANES), jnp.float32)
    here, there = call(
        far_body,
        [lines, lines],
        2 * HALF * BORDER * width,
        mine,
        other,
        tile,
        near,
    )
    swapped = lax.ppermute(jnp.concatenate([there, here]), "rep", swap)
    totals = jnp.concatenate([here, there]) + swapped
    scores = -jnp.log(totals / (CAP - 1 + BORDER))
    lines = HALF // LANES
    answers = call(
        answer_body,
        jax.ShapeDtypeStruct((rows // LANES, LANES), jnp.float32),
        owners * HALF,
        gather_halves(scores[:lines], scores[lines:]),
        cluster_of.reshape(rows // LANES, LANES),
        order_in.reshape(rows // LANES, LANES),
        base,
    )
    return answers.reshape(rows)


def solution(mesh):
    return jax.shard_map(
        per_device,
        mesh=mesh,
        in_specs=(
            P(("groups", "clus", "sub", "rep"), None),
            P(("groups", "clus", "sub", "rep")),
            P(("groups", "clus", "sub", "rep")),
            P(("groups", "clus", "sub")),
            P(("groups", "clus", "sub"), None),
        ),
        out_specs=P(("groups", "clus", "sub", "rep")),
        check_vma=False,
    )
```

```python
import functools
import math

import jax
import jax.numpy as jnp
from jax import lax
from jax.experimental import pallas as pl
from jax.experimental.pallas import tpu as pltpu
from jax.sharding import PartitionSpec as P

CAP = 1024
HALF = CAP // 2
BORDER = 256
EPS = 1e-06
SCALE = 0.1
LANES = 128
TAG_ROWS = 8
TAG_BASE = 32
EMPTY = 4096
PIECES = (64, 112, 112, 112, 112)
OWNERS = ("clus", "sub")

ROWS_BY_ROWS = (((1,), (1,)), ((), ()))


def dot(a, b, dims=(((1,), (0,)), ((), ()))):
    return lax.dot_general(a, b, dims, preferred_element_type=jnp.float32)


def call(body, out_shape, flops, *args, after=()):
    leaves, tree = jax.tree.flatten(args)
    moved = sum(a.size * a.dtype.itemsize for a in leaves)
    moved += sum(o.size * o.dtype.itemsize for o in jax.tree.leaves(out_shape))
    spec = pl.BlockSpec(memory_space=pltpu.VMEM)
    many = isinstance(out_shape, (list, tuple))
    count = len(leaves)

    def kernel(*refs):
        body(*jax.tree.unflatten(tree, refs[:count]), *refs[count + len(after) :])

    return pl.pallas_call(
        kernel,
        out_shape=out_shape,
        in_specs=[spec] * count + [pl.BlockSpec(memory_space=pl.ANY)] * len(after),
        out_specs=[spec] * len(out_shape) if many else spec,
        compiler_params=pltpu.CompilerParams(vmem_limit_bytes=40 * 2**20),
        cost_estimate=pl.CostEstimate(
            flops=flops, bytes_accessed=moved if flops else 0, transcendentals=0
        ),
    )(*leaves, *after)


def iota(shape, axis):
    return lax.broadcasted_iota(jnp.int32, shape, axis)


def one_hot(condition):
    return jnp.where(condition, 1.0, 0.0).astype(jnp.bfloat16)


TAGS = {
    0: ((0,), ()),
    1: ((1, 3, 7, 5), ()),
    2: ((2, 4), ((1, 1), (1, 3))),
    6: ((6,), ((1, 2), (2, 1), (2, 3))),
}
TAG_LINE = ((0, 0), (1, 0), (2, 0), (2, 2), (6, 2), (6, 3), (6, 0), (6, 1))
STEPS = (((7, 4), ()), ((1, 0), ()), ((2, 5), (1,)), ((6, 3), (1, 2)))


BELOW = {0: TAG_ROWS, 1: 6 * TAG_ROWS, 2: 6 * TAG_ROWS, 6: TAG_ROWS}


def chunk_shape(block, send, width):
    if block in TAGS:
        return width // LANES * send + BELOW[block], LANES
    return send, width


def rows_in(chunk, send):
    if chunk.shape[0] == send:
        return chunk[...]
    columns = [chunk[n : n + send, :] for n in range(0, chunk.shape[0] - send + 1, send)]
    return jnp.concatenate(columns, axis=1)


def digits_in(chunk, send):
    first = chunk.shape[0] // send * send
    return chunk[first : first + TAG_ROWS, :].astype(jnp.float32)


def pack(send, blocks, unit, place, position, arrived, outs):
    rows, width = unit.shape
    if position is not None:
        parts = jnp.where(iota((16, rows), 0) == 0, position // TAG_BASE, position % TAG_BASE)
        parts = parts.astype(jnp.float32).astype(jnp.bfloat16)
    digits = {k: digits_in(ref, send) for k, ref in arrived.items()}

    def chosen(block):
        return one_hot(iota((send, rows), 0) + block * send == place)

    for block, out in zip(blocks, outs):
        packed = dot(chosen(block), unit).astype(jnp.bfloat16)
        if block not in TAGS:
            out[...] = packed
            continue
        for n in range(width // LANES):
            out[n * send : (n + 1) * send, :] = packed[:, n * LANES : (n + 1) * LANES]
        own, handed = TAGS[block]
        lines = []
        for b in own:
            found = dot(parts, chosen(b), ROWS_BY_ROWS)
            lines.append((found[0:1], found[1:2]))
        for c, n in handed:
            lines.append((digits[c][n : n + 1], digits[c][n + TAG_ROWS // 2 :][:1]))
        lines += [(jnp.zeros((1, send), jnp.float32),) * 2] * (TAG_ROWS // 2 - len(lines))
        lines = [high for high, _ in lines] + [low for _, low in lines]
        rest = jnp.zeros((BELOW[block] - TAG_ROWS, send), jnp.float32)
        lines = jnp.concatenate([*lines, rest] if rest.size else lines, axis=0)
        out[width // LANES * send :, :] = lines.astype(jnp.bfloat16)


def steps_body(steps_ref):
    steps_ref[...] = one_hot(iota(steps_ref.shape, 0) % LANES < iota(steps_ref.shape, 1))
    steps_ref[LANES:, :] = jnp.ones((LANES, LANES), jnp.bfloat16)


def ranks(which, steps):
    lines, rows = which.shape
    hits = jnp.where(which, 1.0, 0.0)
    sums = jnp.zeros((lines, LANES), jnp.float32)
    parts, totals = [], []
    for n in range(0, rows, LANES):
        parts.append(hits[:, n : n + LANES])
        totals.append(sums)
        sums = sums + parts[-1]
    both = [jnp.concatenate(x, axis=0).astype(jnp.bfloat16) for x in (parts, totals)]
    found = dot(jnp.concatenate(both, axis=1), steps)
    return jnp.concatenate([found[n : n + lines] for n in range(0, found.shape[0], lines)], axis=1)


def place_of_body(owners, send, steps_ref, cluster_ref, base_ref, place_ref):
    owner = cluster_ref[...] ^ base_ref[...]
    which = iota((max(owners, 16), cluster_ref.shape[1]), 0) == owner
    rank = jnp.sum(jnp.where(which, ranks(which, steps_ref[...]), 0.0), axis=0, keepdims=True)
    place_ref[...] = owner * send + rank.astype(jnp.int32)


def first_body(send, blocks, embeds_ref, place_ref, unit_ref, *outs):
    values = embeds_ref[...].astype(jnp.float32)
    mean = jnp.sum(values * values, axis=1, keepdims=True) / values.shape[1]
    unit = (values * lax.rsqrt(mean + EPS)).astype(jnp.bfloat16)
    unit_ref[...] = unit
    place = place_ref[...]
    if blocks:
        pack(send, blocks, unit, place, None, {}, outs)
    else:
        (out,) = outs
        chosen = one_hot(iota((out.shape[0], place.shape[1]), 0) == place)
        out[...] = dot(chosen, unit).astype(jnp.bfloat16)


def pack_body(send, blocks, unit_ref, place_ref, order_ref, arrived, *outs):
    position = order_ref[...] % HALF + 1
    pack(send, blocks, unit_ref[...], place_ref[...], position, arrived, outs)


def tags_of(chunks, tags, send):
    if tags:
        return tags[0][...]
    digits = {k: digits_in(chunks[k], send) for k in TAGS}
    found = []
    for k, n in TAG_LINE:
        low = n + TAG_ROWS // 2
        found.append(digits[k][n : n + 1] * TAG_BASE + digits[k][low : low + 1])
    found = jnp.concatenate(found, axis=1).astype(jnp.int32)
    return jnp.where(found == 0, EMPTY, found - 1)


def rows_of(chunks, send):
    if 1 not in chunks:
        return chunks[0][...]
    return jnp.concatenate([rows_in(chunks[k], send) for k in range(8)], axis=0)


def give_body(send, chunks, want_ref, tags, give_ref):
    chosen = one_hot(want_ref[BORDER // 2 :, :] == tags_of(chunks, tags, send))
    give_ref[...] = dot(chosen, rows_of(chunks, send)).astype(jnp.bfloat16)


def keep_body(send, chunks, want_ref, tags, keep_ref, head_ref):
    tags = tags_of(chunks, tags, send)
    first = iota((head_ref.shape[0], tags.shape[1]), 0)
    chosen = [one_hot(want_ref[: BORDER // 2, :] == tags), one_hot(first == tags)]
    chosen = jnp.concatenate(chosen, axis=0)
    picked = dot(chosen, rows_of(chunks, send)).astype(jnp.bfloat16)
    keep_ref[...] = picked[: keep_ref.shape[0]]
    head_ref[...] = picked[keep_ref.shape[0] :]


def place_body(send, chunks, tags, *mine_refs):
    tags = tags_of(chunks, tags, send)
    first = HALF - sum(ref.shape[0] for ref in mine_refs)
    chosen = one_hot(iota((HALF - first, tags.shape[1]), 0) + first == tags)
    placed = dot(chosen, rows_of(chunks, send)).astype(jnp.bfloat16)
    first = 0
    for ref in mine_refs:
        ref[...] = placed[first : first + ref.shape[0]]
        first += ref.shape[0]


def weigh(products, width):
    by = math.log2(math.e) / SCALE
    return jnp.exp2(products * (by / width) - by)


def near_body(mine_refs, other_refs, near_ref):
    mine = jnp.concatenate([ref[...] for ref in mine_refs], axis=0)
    other = jnp.concatenate([ref[...] for ref in other_refs], axis=0)
    width = mine.shape[1]
    own = weigh(dot(mine, mine, ROWS_BY_ROWS), width)
    own = jnp.where(iota(own.shape, 0) == iota(own.shape, 1), 0.0, own)
    across = weigh(dot(other, mine, ROWS_BY_ROWS), width)
    near_ref[...] = jnp.sum(own, axis=0, keepdims=True) + jnp.sum(across, axis=0, keepdims=True)


def far_body(mine_refs, other_refs, tile_ref, near_ref, here_ref, there_ref):
    tile = tile_ref[...]
    for rows_refs, out_ref in ((mine_refs, here_ref), (other_refs, there_ref)):
        rows = jnp.concatenate([ref[...] for ref in rows_refs], axis=0)
        far = weigh(dot(tile, rows, ROWS_BY_ROWS), tile.shape[1])
        total = jnp.sum(far, axis=0, keepdims=True)
        if out_ref is here_ref:
            total = total + near_ref[...]
        for r in range(HALF // LANES):
            out_ref[r : r + 1, :] = total[:, r * LANES : (r + 1) * LANES]


def answer_body(backwards, scores_ref, cluster_ref, order_ref, base_ref, out_ref):
    lines_each = HALF // LANES
    place = order_ref[...] % HALF
    owner = cluster_ref[...] ^ base_ref[...]
    if backwards:
        owner = owner % 2 * 4 + owner // 2 % 2 * 2 + owner // 4
    line = owner * lines_each + place // LANES
    lane = place % LANES

    def add(n, found):
        scores = jnp.broadcast_to(scores_ref[pl.ds(n, 1), :], lane.shape)
        there = jnp.take_along_axis(scores, lane, axis=1)
        return jnp.where(line == n, there, found)

    lines = scores_ref.shape[0]
    found = jnp.zeros(lane.shape, jnp.float32)
    out_ref[...] = lax.fori_loop(0, lines, add, found, unroll=lines <= 64)


def per_device(embeds, cluster_of, order_in, partner, border_idx):
    rows, width = embeds.shape
    clus_count = lax.axis_size("clus")
    owners = clus_count * lax.axis_size("sub")
    send = 2 * rows // owners
    me = lax.axis_index(OWNERS)
    side = lax.axis_index("rep")
    swap = [(0, 1), (1, 0)]
    paired = owners == 8

    def toward(x, flip):
        return lax.ppermute(x, OWNERS, [(i, i ^ flip) for i in range(owners)])

    def across(x, flip):
        pairs = [(2 * i + r, 2 * (i ^ flip) + 1 - r) for i in range(owners) for r in range(2)]
        return lax.ppermute(x, (*OWNERS, "rep"), pairs)

    def gather(x):
        return lax.all_gather(x, OWNERS, axis=0, tiled=True)

    def gather_halves(mine, other):
        if not paired:
            return gather(mine)
        count = mine.shape[0]
        arrived = across(jnp.concatenate([other, mine]), 4)
        mine = jnp.concatenate([mine, arrived[:count]])
        other = jnp.concatenate([other, arrived[count:]])
        return jnp.concatenate([mine] + [across(other, flip) for flip in (2, 1, 3)])

    base = me if paired else jnp.zeros_like(me)
    base = base.reshape(1, 1)
    cluster_row = cluster_of.reshape(1, rows)
    order_row = order_in.reshape(1, rows)

    def shapes(blocks):
        sizes = [chunk_shape(b, send, width) for b in blocks] or [(owners * send, width)]
        return [jax.ShapeDtypeStruct(size, jnp.bfloat16) for size in sizes]

    steps = call(steps_body, jax.ShapeDtypeStruct((2 * LANES, LANES), jnp.bfloat16), 2 * 10**9)
    place = call(
        functools.partial(place_of_body, owners, send),
        jax.ShapeDtypeStruct((1, rows), jnp.int32),
        10**8,
        steps,
        cluster_row,
        base,
    )

    def first(blocks):
        return call(
            functools.partial(first_body, send, blocks),
            [jax.ShapeDtypeStruct((rows, width), jnp.bfloat16), *shapes(blocks)],
            2 * rows * rows * width,
            embeds,
            place,
        )

    if paired:
        chunks = {}
        for blocks, needed in STEPS:
            if not chunks:
                unit, *packed = first(blocks)
            else:
                handed = {k: chunks[k] for k in needed}
                packed = call(
                    functools.partial(pack_body, send, blocks),
                    shapes(blocks),
                    2 * len(blocks) * send * rows * width,
                    unit,
                    place,
                    order_row,
                    handed,
                )
            for block, chunk in zip(blocks, packed):
                chunks[block] = toward(chunk, block) if block else chunk
        tags = []
    else:
        _, blocks = first(())
        blocks = blocks.reshape(owners, send, width)
        blocks = lax.all_to_all(blocks, OWNERS, split_axis=0, concat_axis=0, tiled=True)
        chunks = {0: blocks.reshape(owners * send, width)}
        every = gather(cluster_of * CAP + order_in).reshape(owners, rows)
        mask = (every // CAP) == me
        index = jnp.arange(rows, dtype=jnp.int32)
        before = (index[:, None] < index[None, :]).astype(jnp.bfloat16)
        rank = dot(mask.astype(jnp.bfloat16), before).astype(jnp.int32)
        rank = jnp.where(mask, rank, -1)
        hit = rank[:, None, :] == index[None, :send, None]
        found = jnp.sum(jnp.where(hit, (every % HALF - EMPTY)[:, None, :], 0), axis=2) + EMPTY
        tags = [found.reshape(1, owners * send)]

    by = clus_count // 2
    opposite = [
        (2 * i + r, 2 * ((i + by) % clus_count) + 1 - r) for i in range(clus_count) for r in range(2)
    ]
    want = border_idx.reshape(BORDER, 1) - side * HALF
    want = jnp.where(side == 0, want, jnp.roll(want, BORDER // 2, axis=0))
    part = jax.ShapeDtypeStruct((BORDER // 2, width), jnp.bfloat16)
    pieces = [jax.ShapeDtypeStruct((count, width), jnp.bfloat16) for count in PIECES]
    give = call(
        functools.partial(give_body, send),
        part,
        BORDER * owners * send * width,
        chunks,
        want,
        tags,
    )
    keep, head = call(
        functools.partial(keep_body, send),
        [part, pieces[0]],
        BORDER * owners * send * width,
        chunks,
        want,
        tags,
        after=[give],
    )
    chosen = keep + lax.ppermute(give, "rep", swap)
    tile = lax.ppermute(chosen, ("clus", "rep"), opposite)
    rest = call(
        functools.partial(place_body, send),
        pieces[1:],
        2 * HALF * owners * send * width,
        chunks,
        tags,
        after=[keep],
    )
    mine = [head, *rest]
    other = [lax.ppermute(part, "rep", swap) for part in mine]
    near = call(
        near_body,
        jax.ShapeDtypeStruct((1, HALF), jnp.float32),
        0,
        mine,
        other,
    )
    lines = jax.ShapeDtypeStruct((HALF // LANES, LANES), jnp.float32)
    here, there = call(
        far_body,
        [lines, lines],
        2 * HALF * BORDER * width,
        mine,
        other,
        tile,
        near,
    )
    swapped = lax.ppermute(jnp.concatenate([there, here]), "rep", swap)
    totals = jnp.concatenate([here, there]) + swapped
    scores = -jnp.log(totals / (CAP - 1 + BORDER))
    lines = HALF // LANES
    answers = call(
        functools.partial(answer_body, paired),
        jax.ShapeDtypeStruct((rows // LANES, LANES), jnp.float32),
        owners * HALF,
        gather_halves(scores[:lines], scores[lines:]),
        cluster_of.reshape(rows // LANES, LANES),
        order_in.reshape(rows // LANES, LANES),
        base,
    )
    return answers.reshape(rows)


def solution(mesh):
    return jax.shard_map(
        per_device,
        mesh=mesh,
        in_specs=(
            P(("groups", "clus", "sub", "rep"), None),
            P(("groups", "clus", "sub", "rep")),
            P(("groups", "clus", "sub", "rep")),
            P(("groups", "clus", "sub")),
            P(("groups", "clus", "sub"), None),
        ),
        out_specs=P(("groups", "clus", "sub", "rep")),
        check_vma=False,
    )
```
